32 devices in a mesh: groups: 2 (over y), blk: 8 (over z, x), uly: 2 (over core).
Axes of the slice: x: 2, y: 2, z: 4, core: 2. Of those that a mesh axis runs over, the one named last changes fastest.
Arguments:
- query_proj: bfloat16 [4096, 4096], P(('groups', 'blk', 'uly')), parts along dimension 0, may hold values from -17 to 17
- key_proj: bfloat16 [4096, 512], P(('groups', 'blk', 'uly')), parts along dimension 0, may hold values from -17 to 17
- value_projection: bfloat16 [4096, 512], P(('groups', 'blk', 'uly')), parts along dimension 0, may hold values from -6 to 6
- query_gain: float32 [128], replicated, may hold values from 0.5 to 6
- key_gain: float32 [128], replicated, may hold values from 0.5 to 6
Outputs:
- attended: bfloat16 [4096, 4096], P(('groups', 'blk', 'uly')), parts along dimension 0
The draws below stay inside these ranges and needn't reach their ends.
There are 2 independent parts, one for each index of `groups`. The reference program is written for one: setup_inputs(seed, part) draws one part's arguments, and reference() takes and returns one part's arrays. A program takes and returns all parts, laid end to end along the dimension named above; an argument that names none is the same for every part. Nothing has to cross between parts.
All inputs are finite; a program needn't handle non-finite values.
Results may differ from the reference program's by a relative error of at most 0.0085.
The reference program's roundings to bfloat16 on the way count: a program that leaves them out, or rounds other values in their place, can miss the bound.
Values may be sent and summed in bfloat16 or wider, within the bound.
No kernel may reach another device: no remote copies, remote signals or barrier semaphores. Data moves between devices by JAX's collectives and lax.ppermute only.
A program may use at most 64 MiB of HBM per device.

```python
import math
import jax
import jax.numpy as jnp
from jax import lax

STRETCH_TOKENS = 128
QUERY_HEADS = 32
KEY_VALUE_HEADS = 4
HEAD_SIZE = 128
WINDOW_TOKENS = 128
SEQUENCE_TOKENS = 2048
N_BLK = 8


def flagged_rows(key, row_count, head_count):
    sample = jnp.clip(jax.random.normal(key, (row_count, head_count, HEAD_SIZE), jnp.float32), -6.0, 6.0)
    return sample.reshape(row_count, head_count * HEAD_SIZE)


def gain_table(key, salt):
    own_key = jax.random.fold_in(key, salt)
    scales = jnp.exp(jax.random.uniform(own_key, (HEAD_SIZE,), jnp.float32, math.log(0.5), math.log(2.0)))
    return scales


def draw_query_proj(key, part):
    return flagged_rows(key, SEQUENCE_TOKENS, QUERY_HEADS).astype(jnp.bfloat16)


def draw_key_proj(key, part):
    return flagged_rows(key, SEQUENCE_TOKENS, KEY_VALUE_HEADS).astype(jnp.bfloat16)


def draw_query_gain(key, part):
    return gain_table(key, 101)


def draw_key_gain(key, part):
    return gain_table(key, 202)


def steps_of(stream_key, extent, cuts, least, largest):
    gain, own = 1.0, jax.random.fold_in(stream_key, 6)
    for dim, blocks in cuts:
        draws = jnp.exp(jax.random.uniform(jax.random.fold_in(own, dim), (blocks,), jnp.float32, least / len(cuts), largest / len(cuts)))
        gain = gain * jnp.repeat(draws, extent[dim] // blocks).reshape([-1 if axis == dim else 1 for axis in range(len(extent))])
    return gain


def normal_values(key, shape, width, bound, cuts=(), kind=jnp.bfloat16):
    array = jax.random.normal(key, shape, jnp.float32) * width
    if len(cuts) > 0:
        array = steps_of(key, shape, cuts, -0.22, 0.18) * array
    return jnp.clip(array, min=-bound, max=bound).astype(kind)


def setup_inputs(seed: int = 0, part: int = 0) -> dict:
    key_list = jax.random.split(jax.random.key(seed), 6)
    part_splits = jax.random.split(jax.random.fold_in(key_list[5], part), 6)
    return {
        "query_proj": draw_query_proj(jax.random.fold_in(jax.random.fold_in(key_list[5], part), 71), part),
        "key_proj": draw_key_proj(jax.random.fold_in(jax.random.fold_in(key_list[5], part), 71), part),
        "value_projection": normal_values(part_splits[2], (SEQUENCE_TOKENS, KEY_VALUE_HEADS * HEAD_SIZE), 1.0, 6.0, ((0, 16),)),
        "query_gain": draw_query_gain(jax.random.fold_in(key_list[5], 71), part),
        "key_gain": draw_key_gain(jax.random.fold_in(key_list[5], 71), part),
    }


NEG_FILL = -1e+30
ROPE_BASE = 1000000.0

def rotate_rows(source, scales, positions):
    head_width = scales.shape[0]
    row_count = source.shape[0]
    head_count = source.shape[1] // head_width
    values = source.astype(jnp.float32).reshape(row_count, head_count, head_width)
    mean_square = lax.optimization_barrier(jnp.mean(values * values, axis=-1, keepdims=True))
    normed = values * lax.rsqrt(mean_square + 1e-06) * scales.astype(jnp.float32)
    half_width = head_width // 2
    frequency = jnp.exp(jnp.arange(half_width, dtype=jnp.float32) * (-2.0 * math.log(ROPE_BASE) / head_width))
    angles = positions.astype(jnp.float32)[:, None] * frequency[None, :]
    cosine = jnp.cos(angles)[:, None, :]
    sine = jnp.sin(angles)[:, None, :]
    first_half = normed[..., :half_width]
    second_half = normed[..., half_width:]
    rotated = jnp.concatenate([first_half * cosine - second_half * sine, second_half * cosine + first_half * sine], axis=-1)
    return rotated.reshape(row_count, head_count * head_width).astype(jnp.bfloat16)

def reference(query_proj, key_proj, value_projection, query_gain, key_gain):
    seq_len = SEQUENCE_TOKENS
    stored = jnp.arange(seq_len, dtype=jnp.int32)
    stored_block = stored // STRETCH_TOKENS
    cycle_pos = stored_block // 2
    stretch_id = jnp.where(stored_block % 2 == 0, cycle_pos, 2 * N_BLK - 1 - cycle_pos)
    position = (stretch_id * STRETCH_TOKENS + stored % STRETCH_TOKENS).astype(jnp.int32)
    query_rot = rotate_rows(query_proj, query_gain, position)
    key_rot = rotate_rows(key_proj, key_gain, position)
    natural = jnp.arange(seq_len, dtype=jnp.int32)
    natural_stretch = natural // STRETCH_TOKENS
    stored_slot = jnp.where(natural_stretch < N_BLK, 2 * natural_stretch, 2 * (2 * N_BLK - 1 - natural_stretch) + 1)
    source = (stored_slot * STRETCH_TOKENS + natural % STRETCH_TOKENS).astype(jnp.int32)
    query_sequence = query_rot[source]
    key_sequence = key_rot[source]
    value_sequence = value_projection[source]
    key_padded = jnp.concatenate([jnp.zeros((WINDOW_TOKENS, KEY_VALUE_HEADS * HEAD_SIZE), jnp.bfloat16), key_sequence], axis=0)
    value_padded = jnp.concatenate([jnp.zeros((WINDOW_TOKENS, KEY_VALUE_HEADS * HEAD_SIZE), jnp.bfloat16), value_sequence], axis=0)
    group_count = QUERY_HEADS // KEY_VALUE_HEADS

    def one_stretch(stretch_index):
        starting_row = (stretch_index * STRETCH_TOKENS).astype(jnp.int32)
        query_tile = lax.dynamic_slice_in_dim(query_sequence, starting_row, STRETCH_TOKENS, 0).astype(jnp.float32).reshape(STRETCH_TOKENS, KEY_VALUE_HEADS, group_count, HEAD_SIZE)
        key_tile = lax.dynamic_slice_in_dim(key_padded, starting_row, WINDOW_TOKENS + STRETCH_TOKENS, 0).astype(jnp.float32).reshape(WINDOW_TOKENS + STRETCH_TOKENS, KEY_VALUE_HEADS, HEAD_SIZE)
        value_tile = lax.dynamic_slice_in_dim(value_padded, starting_row, WINDOW_TOKENS + STRETCH_TOKENS, 0).astype(jnp.float32).reshape(WINDOW_TOKENS + STRETCH_TOKENS, KEY_VALUE_HEADS, HEAD_SIZE)
        scores = jnp.einsum('rkgd,nkd->kgrn', query_tile, key_tile) * (1.0 / math.sqrt(HEAD_SIZE))
        query_pos = starting_row + jnp.arange(STRETCH_TOKENS, dtype=jnp.int32)
        key_pos = starting_row - WINDOW_TOKENS + jnp.arange(WINDOW_TOKENS + STRETCH_TOKENS, dtype=jnp.int32)
        distance = query_pos[:, None] - key_pos[None, :]
        allowed = (distance >= 0) & (distance < WINDOW_TOKENS) & (key_pos >= 0)[None, :]
        scores = jnp.where(allowed, scores, NEG_FILL)
        top_score = lax.optimization_barrier(jnp.max(scores, axis=-1, keepdims=True))
        weights = jnp.exp(scores - top_score)
        total_weight = lax.optimization_barrier(jnp.sum(weights, axis=-1))
        rounded = lax.optimization_barrier(weights.astype(jnp.bfloat16)).astype(jnp.float32)
        mixed_rows = jnp.einsum('kgrn,nkd->kgrd', rounded, value_tile) / total_weight[..., None]
        return jnp.transpose(mixed_rows, (2, 0, 1, 3)).reshape(STRETCH_TOKENS, QUERY_HEADS * HEAD_SIZE).astype(jnp.bfloat16)
    stretches = lax.map(one_stretch, jnp.arange(2 * N_BLK, dtype=jnp.int32))
    out_seq = stretches.reshape(seq_len, QUERY_HEADS * HEAD_SIZE)
    return out_seq[position]
```

```python
import functools
import math

import jax
import jax.numpy as jnp
import numpy as np
from jax import lax
from jax.experimental import pallas as pl
from jax.experimental.pallas import tpu as pltpu
from jax.sharding import PartitionSpec as P

NEG_FILL = -1e30
ROPE_BASE = 1000000.0
EPSILON = 1e-06
VMEM_LIMIT = 48 * 1024 * 1024


def stretch_device(stretch, cycle):
    return 2 * stretch if stretch < cycle else 2 * (2 * cycle - 1 - stretch) + 1


def forward_route(distance, cycle):
    total = 2 * cycle
    return [
        (stretch_device(s, cycle), stretch_device((s + distance) % total, cycle))
        for s in range(total)
    ]


def rotary_tables(stretches, length, width):
    half = width // 2
    frequency = ROPE_BASE ** (-2.0 * np.arange(half, dtype=np.float64) / width)
    frequency = np.concatenate([frequency, frequency])
    base = (np.arange(stretches, dtype=np.float64) * length)[:, None] * frequency
    offset = np.arange(length, dtype=np.float64)[:, None] * frequency
    sign = np.where(np.arange(width) < half, -1.0, 1.0)
    base = np.concatenate([np.cos(base), np.sin(base)], axis=1)
    offset = np.stack([np.cos(offset), np.sin(offset), np.cos(offset) * sign, np.sin(offset) * sign])
    return base.astype(np.float32), offset.astype(np.float32)


def my_stretch(cycle):
    block = lax.axis_index("blk")
    return jnp.where(lax.axis_index("uly") == 0, block, 2 * cycle - 1 - block)


def gained_tables(base_ref, offset_ref, gain, stretch):
    width = gain.shape[-1]
    base = base_ref[pl.ds(stretch, 1), :]
    base_cos, base_sin = base[:, :width], base[:, width:]
    cosine = base_cos * offset_ref[0] - base_sin * offset_ref[1]
    sine = base_sin * offset_ref[2] + base_cos * offset_ref[3]
    return gain * cosine, pltpu.roll(gain, width // 2, 1) * sine


def rotate_head(raw, cosine, sine):
    values = raw.astype(jnp.float32)
    width = values.shape[-1]
    mean_square = jnp.sum(values * values, axis=-1, keepdims=True) * (1.0 / width)
    turned = values * cosine + pltpu.roll(values, width // 2, 1) * sine
    return (turned * lax.rsqrt(mean_square + EPSILON)).astype(jnp.bfloat16)


def matmul(left, right):
    return jnp.dot(left, right, preferred_element_type=jnp.float32)


def matmul_t(left, right):
    return lax.dot_general(left, right, (((1,), (1,)), ((), ())), preferred_element_type=jnp.float32)


def local_kernel(
    cycle, span, q_ref, k_ref, q_gain_ref, k_gain_ref, base_ref, offset_ref, rotated_ref, score_ref, table_ref
):
    heads, length, width = rotated_ref.shape
    kv_heads = k_ref.shape[1] // width
    group = heads // kv_heads
    stretch = my_stretch(cycle)
    k_gain = k_gain_ref[...]
    q_cos, q_sin = gained_tables(base_ref, offset_ref, q_gain_ref[...], stretch)
    k_cos, k_sin = gained_tables(base_ref, offset_ref, k_gain, stretch)
    for d in range(1, span + 1):
        before = jnp.maximum(stretch - d, 0)
        table_ref[d - 1, 0], table_ref[d - 1, 1] = gained_tables(base_ref, offset_ref, k_gain, before)
    for g in range(kv_heads):
        keys = rotate_head(k_ref[:, g * width : (g + 1) * width], k_cos, k_sin)
        for h in range(g * group, (g + 1) * group):
            rotated_ref[h] = rotate_head(q_ref[:, h * width : (h + 1) * width], q_cos, q_sin)
        queries = rotated_ref[g * group : (g + 1) * group].reshape(group * length, width)
        score_ref[g * group : (g + 1) * group] = matmul_t(queries, keys).reshape(group, length, length)


def weight_kernel(cycle, span, rotated_ref, score_ref, table_ref, *refs):
    key_refs = refs[:span]
    weight_ref, inverse_ref = refs[span:]
    heads, length, width = rotated_ref.shape
    kv_heads = key_refs[0].shape[1] // width
    group = heads // kv_heads
    stretch = my_stretch(cycle)
    to_exponent = math.log2(math.e) / math.sqrt(width)
    rows = lax.broadcasted_iota(jnp.int32, (length, length), 0)
    columns = lax.broadcasted_iota(jnp.int32, (length, length), 1)
    own = columns <= rows
    own_part = own.astype(jnp.float32).astype(jnp.bfloat16)
    far_part = (1.0 - own.astype(jnp.float32)).astype(jnp.bfloat16)
    absent = [jnp.where(stretch >= d, 0.0, NEG_FILL).astype(jnp.float32) for d in range(1, span + 1)]
    for g in range(kv_heads):
        keys = [
            rotate_head(key_refs[d][:, g * width : (g + 1) * width], table_ref[d, 0], table_ref[d, 1])
            for d in range(span)
        ]
        queries = rotated_ref[g * group : (g + 1) * group].reshape(group * length, width)
        far = [matmul_t(queries, keys[d]).reshape(group, length, length) for d in range(span)]
        for i in range(group):
            h = g * group + i
            tiles = [jnp.where(own, score_ref[h], far[span - 1][i] + absent[span - 1])]
            tiles += [far[d][i] + absent[d] for d in range(span - 1)]
            top = functools.reduce(jnp.maximum, tiles)
            top = jnp.max(top, axis=-1, keepdims=True)
            weights = [jnp.exp2((tile - top) * to_exponent) for tile in tiles]
            total = jnp.sum(functools.reduce(jnp.add, weights), axis=-1, keepdims=True)
            inverse_ref[h] = jnp.broadcast_to(1.0 / total, (length, width))
            rounded = [w.astype(jnp.bfloat16) for w in weights]
            weight_ref[h, :, :length] = rounded[0] * own_part
            for d in range(span - 1):
                weight_ref[h, :, (d + 1) * length : (d + 2) * length] = rounded[d + 1]
            weight_ref[h, :, span * length :] = rounded[0] * far_part


def mix_kernel(span, weight_ref, inverse_ref, *refs):
    value_refs = refs[: span + 1]
    out_ref, held_ref, stage_ref, in_sem, out_sem = refs[span + 1 :]
    heads, length, keys = weight_ref.shape
    kv_heads, _, width = held_ref.shape
    group = heads // kv_heads
    fetches = []
    for g in range(kv_heads):
        for d in range(span + 1):
            fetches.append(
                pltpu.make_async_copy(
                    value_refs[d].at[:, g * width : (g + 1) * width],
                    held_ref.at[g, d * length : (d + 1) * length],
                    in_sem.at[g, d],
                )
            )
            fetches[-1].start()
    stores = []
    for g in range(kv_heads):
        for d in range(span + 1):
            fetches[g * (span + 1) + d].wait()
        weights = weight_ref[g * group : (g + 1) * group].reshape(group * length, keys)
        mixed = matmul(weights, held_ref[g]).reshape(group, length, width)
        for i in range(group):
            h = g * group + i
            stage_ref[:, h * width : (h + 1) * width] = (mixed[i] * inverse_ref[h]).astype(jnp.bfloat16)
        block = slice(g * group * width, (g + 1) * group * width)
        stores.append(pltpu.make_async_copy(stage_ref.at[:, block], out_ref.at[:, block], out_sem.at[g]))
        stores[-1].start()
    for store in stores:
        store.wait()


def local(query_proj, key_proj, value_projection, query_gain, key_gain):
    cycle = lax.axis_size("blk")
    span = max(1, cycle // 64)
    length, query_width = query_proj.shape
    width = query_gain.shape[0]
    heads = query_width // width
    kv_heads = key_proj.shape[1] // width
    params = pltpu.CompilerParams(vmem_limit_bytes=VMEM_LIMIT)
    vmem = pl.BlockSpec(memory_space=pltpu.VMEM)
    hbm = pl.BlockSpec(memory_space=pltpu.HBM)

    routes = [forward_route(d, cycle) for d in range(1, span + 1)]
    far_keys = [lax.ppermute(key_proj, ("blk", "uly"), route) for route in routes]
    far_values = [lax.ppermute(value_projection, ("blk", "uly"), route) for route in routes]

    base, offset = rotary_tables(2 * cycle, length, width)
    rotated, scores, tables = pl.pallas_call(
        functools.partial(local_kernel, cycle, span),
        in_specs=[vmem] * 6,
        out_specs=[vmem] * 3,
        out_shape=[
            pltpu.VMEM((heads, length, width), jnp.bfloat16),
            pltpu.VMEM((heads, length, length), jnp.float32),
            pltpu.VMEM((span, 2, length, width), jnp.float32),
        ],
        compiler_params=params,
        name="local_scores",
    )(query_proj, key_proj, query_gain[None], key_gain[None], base, offset)
    weights, inverse = pl.pallas_call(
        functools.partial(weight_kernel, cycle, span),
        in_specs=[vmem] * (3 + span),
        out_specs=[vmem] * 2,
        out_shape=[
            pltpu.VMEM((heads, length, (span + 1) * length), jnp.bfloat16),
            pltpu.VMEM((heads, length, width), jnp.float32),
        ],
        compiler_params=params,
        name="weights",
    )(rotated, scores, tables, *far_keys)
    return pl.pallas_call(
        functools.partial(mix_kernel, span),
        in_specs=[vmem] * 2 + [hbm] * (span + 1),
        out_specs=hbm,
        out_shape=jax.ShapeDtypeStruct(query_proj.shape, jnp.bfloat16),
        scratch_shapes=[
            pltpu.VMEM((kv_heads, (span + 1) * length, width), jnp.bfloat16),
            pltpu.VMEM(query_proj.shape, jnp.bfloat16),
            pltpu.SemaphoreType.DMA((kv_heads, span + 1)),
            pltpu.SemaphoreType.DMA((kv_heads,)),
        ],
        compiler_params=params,
        name="mix_values",
    )(weights, inverse, value_projection, *far_values)


def solution(mesh):
    placed = P(("groups", "blk", "uly"), None)
    return jax.shard_map(
        local,
        mesh=mesh,
        in_specs=(placed, placed, placed, P(), P()),
        out_specs=placed,
        check_vma=False,
    )
```

```python
import functools
import math

import jax
import jax.numpy as jnp
import numpy as np
from jax import lax
from jax.experimental import pallas as pl
from jax.experimental.pallas import tpu as pltpu
from jax.sharding import PartitionSpec as P

NEG_FILL = -1e30
ROPE_BASE = 1000000.0
EPSILON = 1e-06
VMEM_LIMIT = 16 * 1024 * 1024


def stretch_device(stretch, cycle):
    return 2 * stretch if stretch < cycle else 2 * (2 * cycle - 1 - stretch) + 1


def forward_route(distance, cycle):
    total = 2 * cycle
    return [
        (stretch_device(s, cycle), stretch_device((s + distance) % total, cycle))
        for s in range(total)
    ]


def rotary_tables(stretches, length, width):
    half = width // 2
    frequency = ROPE_BASE ** (-2.0 * np.arange(half, dtype=np.float64) / width)
    frequency = np.concatenate([frequency, frequency])
    base = (np.arange(stretches, dtype=np.float64) * length)[:, None] * frequency
    offset = np.arange(length, dtype=np.float64)[:, None] * frequency
    sign = np.where(np.arange(width) < half, -1.0, 1.0)
    base = np.concatenate([np.cos(base), np.sin(base)], axis=1)
    offset = np.stack([np.cos(offset), np.sin(offset), np.cos(offset) * sign, np.sin(offset) * sign])
    return base.astype(np.float32), offset.astype(np.float32)


def my_stretch(cycle):
    block = lax.axis_index("blk")
    return jnp.where(lax.axis_index("uly") == 0, block, 2 * cycle - 1 - block)


def gained_tables(base_ref, offset_ref, gain, stretch):
    width = gain.shape[-1]
    base = base_ref[pl.ds(stretch, 1), :]
    base_cos, base_sin = base[:, :width], base[:, width:]
    cosine = base_cos * offset_ref[0] - base_sin * offset_ref[1]
    sine = base_sin * offset_ref[2] + base_cos * offset_ref[3]
    return gain * cosine, pltpu.roll(gain, width // 2, 1) * sine


def rotate_head(raw, cosine, sine):
    values = raw.astype(jnp.float32)
    width = values.shape[-1]
    mean_square = jnp.sum(values * values, axis=-1, keepdims=True) * (1.0 / width)
    turned = values * cosine + pltpu.roll(values, width // 2, 1) * sine
    return (turned * lax.rsqrt(mean_square + EPSILON)).astype(jnp.bfloat16)


def matmul(left, right):
    return jnp.dot(left, right, preferred_element_type=jnp.float32)


def matmul_t(left, right):
    return lax.dot_general(left, right, (((1,), (1,)), ((), ())), preferred_element_type=jnp.float32)


def local_kernel(
    cycle,
    span,
    q_hbm,
    k_hbm,
    v_hbm,
    q_gain_hbm,
    k_gain_hbm,
    base_hbm,
    offset_hbm,
    rotated_ref,
    score_ref,
    table_ref,
    value_ref,
    q_ref,
    k_ref,
    q_gain_ref,
    k_gain_ref,
    base_ref,
    offset_ref,
    small_sem,
    q_sem,
    v_sem,
):
    heads, length, width = rotated_ref.shape
    kv_heads = k_ref.shape[1] // width
    group = heads // kv_heads
    stretch = my_stretch(cycle)
    smalls = [
        pltpu.make_async_copy(source, target, small_sem.at[i])
        for i, (source, target) in enumerate(
            [
                (q_gain_hbm, q_gain_ref),
                (k_gain_hbm, k_gain_ref),
                (base_hbm, base_ref),
                (offset_hbm, offset_ref),
                (k_hbm, k_ref),
            ]
        )
    ]
    for copy in smalls:
        copy.start()
    q_copies = []
    for g in range(kv_heads):
        block = slice(g * group * width, (g + 1) * group * width)
        q_copies.append(pltpu.make_async_copy(q_hbm.at[:, block], q_ref.at[:, block], q_sem.at[g]))
        q_copies[-1].start()
    v_copy = pltpu.make_async_copy(v_hbm, value_ref, v_sem)
    v_copy.start()
    for copy in smalls:
        copy.wait()

    k_gain = k_gain_ref[...]
    q_cos, q_sin = gained_tables(base_ref, offset_ref, q_gain_ref[...], stretch)
    k_cos, k_sin = gained_tables(base_ref, offset_ref, k_gain, stretch)
    for d in range(1, span + 1):
        before = jnp.maximum(stretch - d, 0)
        table_ref[d - 1, 0], table_ref[d - 1, 1] = gained_tables(base_ref, offset_ref, k_gain, before)
    rows = lax.broadcasted_iota(jnp.int32, (length, length), 0)
    columns = lax.broadcasted_iota(jnp.int32, (length, length), 1)
    own = columns <= rows
    for g in range(kv_heads):
        keys = rotate_head(k_ref[:, g * width : (g + 1) * width], k_cos, k_sin)
        q_copies[g].wait()
        for h in range(g * group, (g + 1) * group):
            rotated_ref[h] = rotate_head(q_ref[:, h * width : (h + 1) * width], q_cos, q_sin)
        queries = rotated_ref[g * group : (g + 1) * group].reshape(group * length, width)
        scores = matmul_t(queries, keys).reshape(group, length, length)
        for i in range(group):
            score_ref[g * group + i] = jnp.where(own, scores[i], NEG_FILL)
    v_copy.wait()


def weight_kernel(cycle, span, rotated_ref, score_ref, table_ref, *refs):
    key_refs = refs[:span]
    weight_ref = refs[span]
    heads, length, width = rotated_ref.shape
    kv_heads = key_refs[0].shape[1] // width
    group = heads // kv_heads
    stretch = my_stretch(cycle)
    to_exponent = math.log2(math.e) / math.sqrt(width)
    rows = lax.broadcasted_iota(jnp.int32, (length, length), 0)
    columns = lax.broadcasted_iota(jnp.int32, (length, length), 1)
    own = columns <= rows
    near = columns <= jnp.where(stretch >= span, rows, length)
    for g in range(kv_heads):
        keys = [
            rotate_head(key_refs[d][:, g * width : (g + 1) * width], table_ref[d, 0], table_ref[d, 1])
            for d in range(span)
        ]
        queries = rotated_ref[g * group : (g + 1) * group].reshape(group * length, width)
        far = [matmul_t(queries, keys[d]).reshape(group, length, length) for d in range(span)]
        for i in range(group):
            h = g * group + i
            tiles = [jnp.where(near, score_ref[h], far[span - 1][i])]
            for d in range(span - 1):
                tiles.append(jnp.where(stretch > d, far[d][i], NEG_FILL))
            top = jnp.max(functools.reduce(jnp.maximum, tiles), axis=-1, keepdims=True)
            weights = [jnp.exp2((tile - top) * to_exponent) for tile in tiles]
            weight_ref[h, :, :length] = jnp.where(own, weights[0], 0.0).astype(jnp.bfloat16)
            for d in range(span - 1):
                weight_ref[h, :, (d + 1) * length : (d + 2) * length] = weights[d + 1].astype(jnp.bfloat16)
            weight_ref[h, :, span * length :] = jnp.where(own, 0.0, weights[0]).astype(jnp.bfloat16)


def mix_kernel(parts, weight_ref, *refs):
    out_hbm, stage_ref, out_sem = refs[-3:]
    value_refs = refs[:-3]
    heads, length, keys = weight_ref.shape
    width = stage_ref.shape[1] // heads
    kv_heads = value_refs[0].shape[1] // width
    group = heads // kv_heads
    step = group // parts
    ones = jnp.ones((keys, width), jnp.bfloat16)
    stores = []
    for g in range(kv_heads):
        values = jnp.concatenate([ref[:, g * width : (g + 1) * width] for ref in value_refs], axis=0)
        values = jnp.concatenate([values, ones], axis=1)
        for first in range(g * group, (g + 1) * group, step):
            weights = weight_ref[first : first + step].reshape(step * length, keys)
            mixed = matmul(weights, values)
            mixed = mixed[:, :width] * (1.0 / mixed[:, width:])
            for i in range(step):
                h = first + i
                stage_ref[:, h * width : (h + 1) * width] = mixed[i * length : (i + 1) * length].astype(jnp.bfloat16)
            block = slice(first * width, (first + step) * width)
            stores.append(
                pltpu.make_async_copy(stage_ref.at[:, block], out_hbm.at[:, block], out_sem.at[first // step])
            )
            stores[-1].start()
    for store in stores:
        store.wait()


def local(query_proj, key_proj, value_projection, query_gain, key_gain):
    cycle = lax.axis_size("blk")
    span = max(1, cycle // 64)
    length, query_width = query_proj.shape
    kv_width = key_proj.shape[1]
    width = query_gain.shape[0]
    heads = query_width // width
    kv_heads = kv_width // width
    params = pltpu.CompilerParams(vmem_limit_bytes=VMEM_LIMIT)
    vmem = pl.BlockSpec(memory_space=pltpu.VMEM)
    hbm = pl.BlockSpec(memory_space=pltpu.HBM)

    routes = [forward_route(d, cycle) for d in range(1, span + 1)]
    far_keys = [lax.ppermute(key_proj, ("blk", "uly"), route) for route in routes]
    far_values = [lax.ppermute(value_projection, ("blk", "uly"), route) for route in routes]

    base, offset = rotary_tables(2 * cycle, length, width)
    operands = (query_proj, key_proj, value_projection, query_gain[None], key_gain[None], base, offset)
    rotated, scores, tables, values = pl.pallas_call(
        functools.partial(local_kernel, cycle, span),
        in_specs=[hbm] * 7,
        out_specs=[vmem] * 4,
        out_shape=[
            pltpu.VMEM((heads, length, width), jnp.bfloat16),
            pltpu.VMEM((heads, length, length), jnp.float32),
            pltpu.VMEM((span, 2, length, width), jnp.float32),
            pltpu.VMEM((length, kv_width), jnp.bfloat16),
        ],
        scratch_shapes=[
            pltpu.VMEM((length, query_width), jnp.bfloat16),
            pltpu.VMEM((length, kv_width), jnp.bfloat16),
            pltpu.VMEM((1, width), jnp.float32),
            pltpu.VMEM((1, width), jnp.float32),
            pltpu.VMEM(base.shape, jnp.float32),
            pltpu.VMEM(offset.shape, jnp.float32),
            pltpu.SemaphoreType.DMA((5,)),
            pltpu.SemaphoreType.DMA((kv_heads,)),
            pltpu.SemaphoreType.DMA,
        ],
        compiler_params=params,
        name="local_scores",
    )(*[pltpu.with_memory_space_constraint(x, pltpu.HBM) for x in operands])
    weights = pl.pallas_call(
        functools.partial(weight_kernel, cycle, span),
        in_specs=[vmem] * (3 + span),
        out_specs=vmem,
        out_shape=pltpu.VMEM((heads, length, (span + 1) * length), jnp.bfloat16),
        compiler_params=params,
        name="weights",
    )(rotated, scores, tables, *far_keys)
    parts = 2 if heads // kv_heads % 2 == 0 else 1
    return pl.pallas_call(
        functools.partial(mix_kernel, parts),
        in_specs=[vmem] * (2 + span),
        out_specs=hbm,
        out_shape=jax.ShapeDtypeStruct(query_proj.shape, jnp.bfloat16),
        scratch_shapes=[
            pltpu.VMEM(query_proj.shape, jnp.bfloat16),
            pltpu.SemaphoreType.DMA((kv_heads * parts,)),
        ],
        compiler_params=params,
        name="mix_values",
    )(weights, values, *far_values)


def solution(mesh):
    placed = P(("groups", "blk", "uly"), None)
    return jax.shard_map(
        local,
        mesh=mesh,
        in_specs=(placed, placed, placed, P(), P()),
        out_specs=placed,
        check_vma=False,
    )
```

```python
import functools
import math

import jax
import jax.numpy as jnp
import numpy as np
from jax import lax
from jax.experimental import pallas as pl
from jax.experimental.pallas import tpu as pltpu
from jax.sharding import PartitionSpec as P

NEG_FILL = -1e30
ROPE_BASE = 1000000.0
EPSILON = 1e-06
DOT_HEADS = 4
LOOP_A, LOOP_B, LOOP_C = False, False, False
VMEM_LIMIT = 16 * 1024 * 1024


def stretch_device(stretch, cycle):
    return 2 * stretch if stretch < cycle else 2 * (2 * cycle - 1 - stretch) + 1


def forward_route(distance, cycle):
    total = 2 * cycle
    return [
        (stretch_device(s, cycle), stretch_device((s + distance) % total, cycle))
        for s in range(total)
    ]


def rotary_tables(stretches, span, length, width):
    half = width // 2
    frequency = ROPE_BASE ** (-2.0 * np.arange(half, dtype=np.float64) / width)
    before = np.maximum(np.arange(stretches)[:, None] - np.arange(span + 1), 0).astype(np.float64)
    base = (before * length)[:, :, None] * frequency
    offset = np.arange(length, dtype=np.float64)[:, None] * frequency
    base = np.concatenate([np.cos(base), np.sin(base)], axis=-1)
    offset = np.concatenate([np.cos(offset), np.sin(offset)], axis=-1)
    return base.astype(np.float32), offset.astype(np.float32)


def my_stretch(cycle):
    block = lax.axis_index("blk")
    return jnp.where(lax.axis_index("uly") == 0, block, 2 * cycle - 1 - block)


def spread(packed):
    half = packed.shape[-1] // 2
    first = lax.broadcasted_iota(jnp.int32, packed.shape, 1) < half
    turned = pltpu.roll(packed, half, 1)
    return jnp.where(first, packed, turned), jnp.where(first, turned, packed)


def gained_tables(base, offset, gain):
    width = gain.shape[-1]
    half = width // 2
    gain = gain * math.sqrt(width)
    turned_gain = pltpu.roll(gain, half, 1)
    turned_gain = jnp.where(lax.broadcasted_iota(jnp.int32, gain.shape, 1) < half, -turned_gain, turned_gain)
    (base_cos, base_sin), (cosine, sine) = base, offset
    return gain * (base_cos * cosine - base_sin * sine), turned_gain * (base_sin * cosine + base_cos * sine)


def rotate_head(raw, cosine, sine):
    values = raw.astype(jnp.float32)
    width = values.shape[-1]
    square_sum = jnp.sum(values * values, axis=-1, keepdims=True)
    turned = values * cosine + pltpu.roll(values, width // 2, 1) * sine
    return (turned * lax.rsqrt(square_sum + width * EPSILON)).astype(jnp.bfloat16)


def columns_of(block, width):
    if isinstance(block, int):
        return slice(block * width, (block + 1) * width)
    return pl.ds(pl.multiple_of(block * width, width), width)


def loop(rolled, count, body):
    if rolled:
        lax.fori_loop(0, count, body, None)
    else:
        for g in range(count):
            body(g, None)


def matmul(left, right):
    return jnp.dot(left, right, preferred_element_type=jnp.float32)


def matmul_t(left, right):
    return lax.dot_general(left, right, (((1,), (1,)), ((), ())), preferred_element_type=jnp.float32)


def local_kernel(
    cycle,
    span,
    q_hbm,
    k_hbm,
    v_hbm,
    q_gain_hbm,
    k_gain_hbm,
    base_hbm,
    offset_hbm,
    rotated_ref,
    score_ref,
    table_ref,
    value_ref,
    q_ref,
    k_ref,
    q_gain_ref,
    k_gain_ref,
    base_ref,
    offset_ref,
    small_sem,
    q_sem,
    v_sem,
):
    heads, length, width = rotated_ref.shape
    kv_heads = k_ref.shape[1] // width
    group = heads // kv_heads
    stretch = my_stretch(cycle)
    smalls = [
        pltpu.make_async_copy(source, target, small_sem.at[i])
        for i, (source, target) in enumerate(
            [
                (q_gain_hbm, q_gain_ref),
                (k_gain_hbm, k_gain_ref),
                (base_hbm.at[stretch], base_ref),
                (offset_hbm, offset_ref),
                (k_hbm, k_ref),
            ]
        )
    ]
    for copy in smalls:
        copy.start()

    def q_copy(g):
        return pltpu.make_async_copy(q_hbm.at[:, columns_of(g, group * width)], q_ref.at[g], q_sem.at[g])

    for g in range(kv_heads):
        q_copy(g).start()
    v_copy = pltpu.make_async_copy(v_hbm, value_ref, v_sem)
    v_copy.start()
    for copy in smalls:
        copy.wait()

    k_gain = k_gain_ref[...]
    bases = [spread(base_ref[d : d + 1]) for d in range(span + 1)]
    offset = spread(offset_ref[...])
    q_cos, q_sin = gained_tables(bases[0], offset, q_gain_ref[...])
    k_cos, k_sin = gained_tables(bases[0], offset, k_gain)
    for d in range(span):
        table_ref[d, 0], table_ref[d, 1] = gained_tables(bases[d + 1], offset, k_gain)
    rows = lax.broadcasted_iota(jnp.int32, (length, length), 0)
    columns = lax.broadcasted_iota(jnp.int32, (length, length), 1)
    own = columns <= rows
    keys = [rotate_head(k_ref[:, columns_of(g, width)], k_cos, k_sin) for g in range(kv_heads)]

    def score(g):
        for i in range(group):
            scores = matmul_t(rotated_ref[g * group + i], keys[g])
            score_ref[g * group + i] = jnp.where(own, scores, NEG_FILL)

    for g in range(kv_heads):
        q_copy(g).wait()
        for i in range(group):
            rotated_ref[g * group + i] = rotate_head(q_ref[g, :, i * width : (i + 1) * width], q_cos, q_sin)
        if g > 0:
            score(g - 1)
    score(kv_heads - 1)
    v_copy.wait()


def weight_kernel(cycle, span, rotated_ref, score_ref, table_ref, *refs):
    key_refs = refs[:span]
    weight_ref = refs[span]
    heads, length, width = rotated_ref.shape
    kv_heads = key_refs[0].shape[1] // width
    group = heads // kv_heads
    stretch = my_stretch(cycle)
    to_exponent = math.log2(math.e) / math.sqrt(width)
    rows = lax.broadcasted_iota(jnp.int32, (length, length), 0)
    columns = lax.broadcasted_iota(jnp.int32, (length, length), 1)
    own = columns <= rows
    near = columns <= jnp.where(stretch >= span, rows, length)

    def one_group(g, carry):
        keys = [
            rotate_head(key_refs[d][:, columns_of(g, width)], table_ref[d, 0], table_ref[d, 1]) for d in range(span)
        ]
        for i in range(group):
            h = g * group + i
            far = [matmul_t(rotated_ref[h], keys[d]) for d in range(span)]
            tiles = [jnp.where(near, score_ref[h], far[span - 1])]
            for d in range(span - 1):
                tiles.append(jnp.where(stretch > d, far[d], NEG_FILL))
            top = jnp.max(functools.reduce(jnp.maximum, tiles), axis=-1, keepdims=True)
            weights = [jnp.exp2((tile - top) * to_exponent) for tile in tiles]
            weights = [jnp.where(own, weights[0], 0.0), *weights[1:], jnp.where(own, 0.0, weights[0])]
            weight_ref[h] = jnp.concatenate(weights, axis=1).astype(jnp.bfloat16)
        return carry

    loop(LOOP_B, kv_heads, one_group)


def mix_kernel(weight_ref, *refs):
    out_hbm, stage_ref, out_sem = refs[-3:]
    value_refs = refs[:-3]
    heads, length, keys = weight_ref.shape
    kv_heads, _, group_width = stage_ref.shape
    group = heads // kv_heads
    width = group_width // group
    ones = jnp.ones((keys, width), jnp.bfloat16)

    def store(g):
        return pltpu.make_async_copy(stage_ref.at[g], out_hbm.at[:, columns_of(g, group_width)], out_sem.at[g])

    def one_group(g, carry):
        values = jnp.concatenate([ref[:, columns_of(g, width)] for ref in value_refs], axis=0)
        values = jnp.concatenate([values, ones], axis=1)
        for first in range(0, group, DOT_HEADS):
            weights = weight_ref[g * group + first : g * group + first + DOT_HEADS]
            mixed = matmul(weights.reshape(DOT_HEADS * length, keys), values)
            mixed = mixed[:, :width] * (1.0 / mixed[:, width:])
            for i in range(DOT_HEADS):
                stage_ref[g, :, columns_of(first + i, width)] = mixed[i * length : (i + 1) * length].astype(jnp.bfloat16)
        store(g).start()
        return carry

    loop(LOOP_C, kv_heads, one_group)
    for g in range(kv_heads):
        store(g).wait()


def local(query_proj, key_proj, value_projection, query_gain, key_gain):
    cycle = lax.axis_size("blk")
    span = max(1, cycle // 64)
    length, query_width = query_proj.shape
    kv_width = key_proj.shape[1]
    width = query_gain.shape[0]
    heads = query_width // width
    kv_heads = kv_width // width
    params = pltpu.CompilerParams(vmem_limit_bytes=VMEM_LIMIT)
    vmem = pl.BlockSpec(memory_space=pltpu.VMEM)
    hbm = pl.BlockSpec(memory_space=pltpu.HBM)

    routes = [forward_route(d, cycle) for d in range(1, span + 1)]
    far_keys = [lax.ppermute(key_proj, ("blk", "uly"), route) for route in routes]
    far_values = [lax.ppermute(value_projection, ("blk", "uly"), route) for route in routes]

    base, offset = rotary_tables(2 * cycle, span, length, width)
    operands = (query_proj, key_proj, value_projection, query_gain[None], key_gain[None], base, offset)
    rotated, scores, tables, values = pl.pallas_call(
        functools.partial(local_kernel, cycle, span),
        in_specs=[hbm] * 7,
        out_specs=[vmem] * 4,
        out_shape=[
            pltpu.VMEM((heads, length, width), jnp.bfloat16),
            pltpu.VMEM((heads, length, length), jnp.float32),
            pltpu.VMEM((span, 2, length, width), jnp.float32),
            pltpu.VMEM((length, kv_width), jnp.bfloat16),
        ],
        scratch_shapes=[
            pltpu.VMEM((kv_heads, length, query_width // kv_heads), jnp.bfloat16),
            pltpu.VMEM((length, kv_width), jnp.bfloat16),
            pltpu.VMEM((1, width), jnp.float32),
            pltpu.VMEM((1, width), jnp.float32),
            pltpu.VMEM(base.shape[1:], jnp.float32),
            pltpu.VMEM(offset.shape, jnp.float32),
            pltpu.SemaphoreType.DMA((5,)),
            pltpu.SemaphoreType.DMA((kv_heads,)),
            pltpu.SemaphoreType.DMA,
        ],
        compiler_params=params,
        name="local_scores",
    )(*[pltpu.with_memory_space_constraint(x, pltpu.HBM) for x in operands])
    weights = pl.pallas_call(
        functools.partial(weight_kernel, cycle, span),
        in_specs=[vmem] * (3 + span),
        out_specs=vmem,
        out_shape=pltpu.VMEM((heads, length, (span + 1) * length), jnp.bfloat16),
        compiler_params=params,
        name="weights",
    )(rotated, scores, tables, *far_keys)
    return pl.pallas_call(
        mix_kernel,
        in_specs=[vmem] * (2 + span),
        out_specs=hbm,
        out_shape=jax.ShapeDtypeStruct(query_proj.shape, jnp.bfloat16),
        scratch_shapes=[
            pltpu.VMEM((kv_heads, length, query_width // kv_heads), jnp.bfloat16),
            pltpu.SemaphoreType.DMA((kv_heads,)),
        ],
        compiler_params=params,
        name="mix_values",
    )(weights, values, *far_values)


def solution(mesh):
    placed = P(("groups", "blk", "uly"), None)
    return jax.shard_map(
        local,
        mesh=mesh,
        in_specs=(placed, placed, placed, P(), P()),
        out_specs=placed,
        check_vma=False,
    )
```

```python
import functools
import math

import jax
import jax.numpy as jnp
import numpy as np
from jax import lax
from jax.experimental import pallas as pl
from jax.experimental.pallas import tpu as pltpu
from jax.sharding import PartitionSpec as P

NEG_FILL = -1e30
ROPE_BASE = 1000000.0
EPSILON = 1e-06
DOT_HEADS = 4
LAG = 1
LOOP_A, LOOP_B, LOOP_C = False, False, False
VMEM_LIMIT = 16 * 1024 * 1024


def stretch_device(stretch, cycle):
    return 2 * stretch if stretch < cycle else 2 * (2 * cycle - 1 - stretch) + 1


def forward_route(distance, cycle):
    total = 2 * cycle
    return [
        (stretch_device(s, cycle), stretch_device((s + distance) % total, cycle))
        for s in range(total)
    ]


def rotary_tables(stretches, span, length, width):
    half = width // 2
    frequency = ROPE_BASE ** (-2.0 * np.arange(half, dtype=np.float64) / width)
    before = np.maximum(np.arange(stretches)[:, None] - np.arange(span + 1), 0).astype(np.float64)
    base = (before * length)[:, :, None] * frequency
    offset = np.arange(length, dtype=np.float64)[:, None] * frequency
    base = np.concatenate([np.cos(base), np.sin(base)], axis=-1)
    offset = np.concatenate([np.cos(offset), np.sin(offset)], axis=-1)
    return base.astype(np.float32), offset.astype(np.float32)


def my_stretch(cycle):
    block = lax.axis_index("blk")
    return jnp.where(lax.axis_index("uly") == 0, block, 2 * cycle - 1 - block)


def spread(packed):
    half = packed.shape[-1] // 2
    first = lax.broadcasted_iota(jnp.int32, packed.shape, 1) < half
    turned = pltpu.roll(packed, half, 1)
    return jnp.where(first, packed, turned), jnp.where(first, turned, packed)


def gained_tables(base, offset, gain):
    width = gain.shape[-1]
    half = width // 2
    gain = gain * math.sqrt(width)
    turned_gain = pltpu.roll(gain, half, 1)
    turned_gain = jnp.where(lax.broadcasted_iota(jnp.int32, gain.shape, 1) < half, -turned_gain, turned_gain)
    (base_cos, base_sin), (cosine, sine) = base, offset
    return gain * (base_cos * cosine - base_sin * sine), turned_gain * (base_sin * cosine + base_cos * sine)


def half_turn(width):
    rows = lax.broadcasted_iota(jnp.int32, (width, width), 0)
    columns = lax.broadcasted_iota(jnp.int32, (width, width), 1)
    swapped = jnp.where(columns < width // 2, columns + width // 2, columns - width // 2)
    return (rows == swapped).astype(jnp.float32).astype(jnp.bfloat16)


def rotate_head(raw, cosine, sine, swap):
    values = raw.astype(jnp.float32)
    width = values.shape[-1]
    square_sum = jnp.sum(values * values, axis=-1, keepdims=True)
    turned = values * cosine + matmul(raw, swap) * sine
    return (turned * lax.rsqrt(square_sum + width * EPSILON)).astype(jnp.bfloat16)


def columns_of(block, width):
    if isinstance(block, int):
        return slice(block * width, (block + 1) * width)
    return pl.ds(pl.multiple_of(block * width, width), width)


def loop(rolled, count, body):
    if rolled:
        lax.fori_loop(0, count, body, None)
    else:
        for g in range(count):
            body(g, None)


def matmul(left, right):
    return jnp.dot(left, right, preferred_element_type=jnp.float32)


def matmul_t(left, right):
    return lax.dot_general(left, right, (((1,), (1,)), ((), ())), preferred_element_type=jnp.float32)


def start_store(stage_ref, out_hbm, out_sem, g):
    place = columns_of(g, stage_ref.shape[2])
    pltpu.make_async_copy(stage_ref.at[g], out_hbm.at[:, place], out_sem).start()


def wait_stores(stage_ref, out_sem):
    pltpu.make_async_copy(stage_ref, stage_ref, out_sem).wait()


def local_kernel(
    cycle,
    span,
    q_hbm,
    k_hbm,
    v_hbm,
    q_gain_hbm,
    k_gain_hbm,
    base_hbm,
    offset_hbm,
    rotated_ref,
    score_ref,
    table_ref,
    value_ref,
    out_hbm,
    q_ref,
    k_ref,
    q_gain_ref,
    k_gain_ref,
    base_ref,
    offset_ref,
    small_sem,
    q_sem,
    v_sem,
    stage_ref,
    out_sem,
):
    heads, length, width = rotated_ref.shape
    kv_heads = k_ref.shape[1] // width
    group = heads // kv_heads
    stretch = my_stretch(cycle)
    smalls = [
        pltpu.make_async_copy(source, target, small_sem.at[i])
        for i, (source, target) in enumerate(
            [
                (q_gain_hbm, q_gain_ref),
                (k_gain_hbm, k_gain_ref),
                (base_hbm.at[stretch], base_ref),
                (offset_hbm, offset_ref),
                (k_hbm, k_ref),
            ]
        )
    ]
    for copy in smalls:
        copy.start()

    def q_copy(g):
        return pltpu.make_async_copy(q_hbm.at[:, columns_of(g, group * width)], q_ref.at[g], q_sem.at[g])

    for g in range(kv_heads):
        q_copy(g).start()
    v_copy = pltpu.make_async_copy(v_hbm, value_ref, v_sem)
    v_copy.start()
    for copy in smalls:
        copy.wait()

    k_gain = k_gain_ref[...]
    bases = [spread(base_ref[d : d + 1]) for d in range(span + 1)]
    offset = spread(offset_ref[...])
    q_cos, q_sin = gained_tables(bases[0], offset, q_gain_ref[...])
    k_cos, k_sin = gained_tables(bases[0], offset, k_gain)
    for d in range(span):
        table_ref[d, 0], table_ref[d, 1] = gained_tables(bases[d + 1], offset, k_gain)
    rows = lax.broadcasted_iota(jnp.int32, (length, length), 0)
    columns = lax.broadcasted_iota(jnp.int32, (length, length), 1)
    own = columns <= rows
    swap = half_turn(width)
    keys = [rotate_head(k_ref[:, columns_of(g, width)], k_cos, k_sin, swap) for g in range(kv_heads)]

    def score(g):
        for i in range(group):
            scores = matmul_t(rotated_ref[g * group + i], keys[g])
            score_ref[g * group + i] = scores

    first = 0
    for count in [2, 2]:
        some = range(first, first + count)
        for g in some:
            q_copy(g).wait()
        for g in some:
            for i in range(group):
                rotated_ref[g * group + i] = rotate_head(q_ref[g, :, i * width : (i + 1) * width], q_cos, q_sin, swap)
        for g in range(max(first - 1, 0), first + count - 1):
            score(g)
        first += count
    score(kv_heads - 1)
    v_copy.wait()

    @pl.when(stretch == 0)
    def _():
        to_exponent = math.log2(math.e) / math.sqrt(width)
        ones = jnp.ones((length, width), jnp.bfloat16)
        for g in range(kv_heads):
            values = jnp.concatenate([value_ref[:, columns_of(g, width)], ones], axis=1)
            for i in range(group):
                tile = jnp.where(own, score_ref[g * group + i], NEG_FILL)
                top = jnp.max(tile, axis=-1, keepdims=True)
                mixed = matmul(jnp.exp2((tile - top) * to_exponent).astype(jnp.bfloat16), values)
                mixed = mixed[:, :width] * (1.0 / mixed[:, width:])
                stage_ref[g, :, columns_of(i, width)] = mixed.astype(jnp.bfloat16)
            start_store(stage_ref, out_hbm, out_sem, g)
        wait_stores(stage_ref, out_sem)


def weight_kernel(cycle, span, *refs):
    @pl.when(my_stretch(cycle) > 0)
    def _():
        later_weights(cycle, span, *refs)


def later_weights(cycle, span, rotated_ref, score_ref, table_ref, *refs):
    key_refs = refs[:span]
    weight_ref = refs[span]
    heads, length, width = rotated_ref.shape
    kv_heads = key_refs[0].shape[1] // width
    group = heads // kv_heads
    stretch = my_stretch(cycle)
    swap = half_turn(width)
    to_exponent = math.log2(math.e) / math.sqrt(width)
    rows = lax.broadcasted_iota(jnp.int32, (length, length), 0)
    columns = lax.broadcasted_iota(jnp.int32, (length, length), 1)
    own = columns <= rows
    near = columns <= jnp.where(stretch >= span, rows, length)

    def scores_of(h, keys):
        far = [matmul_t(rotated_ref[h], key) for key in keys]
        tiles = [jnp.where(near, score_ref[h], far[span - 1])]
        for d in range(span - 1):
            tiles.append(jnp.where(stretch > d, far[d], NEG_FILL))
        return tiles, jnp.max(functools.reduce(jnp.maximum, tiles), axis=-1, keepdims=True)

    def weights_of(h, tiles, top):
        weights = [jnp.exp2((tile - top) * to_exponent) for tile in tiles]
        weights = [jnp.where(own, weights[0], 0.0), *weights[1:], jnp.where(own, 0.0, weights[0])]
        weight_ref[h] = jnp.concatenate(weights, axis=1).astype(jnp.bfloat16)

    keys = [
        [
            rotate_head(key_refs[d][:, columns_of(g, width)], table_ref[d, 0], table_ref[d, 1], swap)
            for d in range(span)
        ]
        for g in range(kv_heads)
    ]
    held = []
    for h in range(heads):
        held.append((h, *scores_of(h, keys[h // group])))
        if len(held) > LAG:
            weights_of(*held.pop(0))
    for item in held:
        weights_of(*item)


def mix_kernel(cycle, weight_ref, *refs):
    out_hbm, stage_ref, out_sem = refs[-3:]
    value_refs = refs[:-4]
    heads, length, keys = weight_ref.shape
    kv_heads, _, group_width = stage_ref.shape
    group = heads // kv_heads
    width = group_width // group

    @pl.when(my_stretch(cycle) > 0)
    def _():
        ones = jnp.ones((keys, width), jnp.bfloat16)
        for g in range(kv_heads):
            values = jnp.concatenate([ref[:, columns_of(g, width)] for ref in value_refs], axis=0)
            values = jnp.concatenate([values, ones], axis=1)
            for first in range(0, group, DOT_HEADS):
                weights = weight_ref[g * group + first : g * group + first + DOT_HEADS]
                mixed = matmul(weights.reshape(DOT_HEADS * length, keys), values)
                mixed = mixed[:, :width] * (1.0 / mixed[:, width:])
                for i in range(DOT_HEADS):
                    part = mixed[i * length : (i + 1) * length].astype(jnp.bfloat16)
                    stage_ref[g, :, columns_of(first + i, width)] = part
            start_store(stage_ref, out_hbm, out_sem, g)
        wait_stores(stage_ref, out_sem)


def local(query_proj, key_proj, value_projection, query_gain, key_gain):
    cycle = lax.axis_size("blk")
    span = max(1, cycle // 64)
    length, query_width = query_proj.shape
    kv_width = key_proj.shape[1]
    width = query_gain.shape[0]
    heads = query_width // width
    kv_heads = kv_width // width
    params = pltpu.CompilerParams(vmem_limit_bytes=VMEM_LIMIT)
    vmem = pl.BlockSpec(memory_space=pltpu.VMEM)
    hbm = pl.BlockSpec(memory_space=pltpu.HBM)

    routes = [forward_route(d, cycle) for d in range(1, span + 1)]
    far_keys = [lax.ppermute(key_proj, ("blk", "uly"), route) for route in routes]
    far_values = [lax.ppermute(value_projection, ("blk", "uly"), route) for route in routes]

    base, offset = rotary_tables(2 * cycle, span, length, width)
    operands = (query_proj, key_proj, value_projection, query_gain[None], key_gain[None], base, offset)
    rotated, scores, tables, values, out = pl.pallas_call(
        functools.partial(local_kernel, cycle, span),
        in_specs=[hbm] * 7,
        out_specs=[vmem] * 4 + [hbm],
        out_shape=[
            pltpu.VMEM((heads, length, width), jnp.bfloat16),
            pltpu.VMEM((heads, length, length), jnp.float32),
            pltpu.VMEM((span, 2, length, width), jnp.float32),
            pltpu.VMEM((length, kv_width), jnp.bfloat16),
            jax.ShapeDtypeStruct(query_proj.shape, jnp.bfloat16),
        ],
        scratch_shapes=[
            pltpu.VMEM((kv_heads, length, query_width // kv_heads), jnp.bfloat16),
            pltpu.VMEM((length, kv_width), jnp.bfloat16),
            pltpu.VMEM((1, width), jnp.float32),
            pltpu.VMEM((1, width), jnp.float32),
            pltpu.VMEM(base.shape[1:], jnp.float32),
            pltpu.VMEM(offset.shape, jnp.float32),
            pltpu.SemaphoreType.DMA((5,)),
            pltpu.SemaphoreType.DMA((kv_heads,)),
            pltpu.SemaphoreType.DMA,
            pltpu.VMEM((kv_heads, length, query_width // kv_heads), jnp.bfloat16),
            pltpu.SemaphoreType.DMA,
        ],
        compiler_params=params,
        name="local_scores",
    )(*[pltpu.with_memory_space_constraint(x, pltpu.HBM) for x in operands])
    weights = pl.pallas_call(
        functools.partial(weight_kernel, cycle, span),
        in_specs=[vmem] * (3 + span),
        out_specs=vmem,
        out_shape=pltpu.VMEM((heads, length, (span + 1) * length), jnp.bfloat16),
        compiler_params=params,
        name="weights",
    )(rotated, scores, tables, *far_keys)
    return pl.pallas_call(
        functools.partial(mix_kernel, cycle),
        in_specs=[vmem] * (2 + span) + [hbm],
        out_specs=hbm,
        out_shape=jax.ShapeDtypeStruct(query_proj.shape, jnp.bfloat16),
        input_output_aliases={2 + span: 0},
        scratch_shapes=[
            pltpu.VMEM((kv_heads, length, query_width // kv_heads), jnp.bfloat16),
            pltpu.SemaphoreType.DMA,
        ],
        compiler_params=params,
        name="mix_values",
    )(weights, values, *far_values, out)


def solution(mesh):
    placed = P(("groups", "blk", "uly"), None)
    return jax.shard_map(
        local,
        mesh=mesh,
        in_specs=(placed, placed, placed, P(), P()),
        out_specs=placed,
        check_vma=False,
    )
```

```python
import functools
import math

import jax
import jax.numpy as jnp
import numpy as np
from jax import lax
from jax.experimental import pallas as pl
from jax.experimental.pallas import tpu as pltpu
from jax.sharding import PartitionSpec as P

NEG_FILL = -1e30
ROPE_BASE = 1000000.0
EPSILON = 1e-06
PAIR = 2
LOOP_A, LOOP_B, LOOP_C = False, False, False
VMEM_LIMIT = 16 * 1024 * 1024


def stretch_device(stretch, cycle):
    return 2 * stretch if stretch < cycle else 2 * (2 * cycle - 1 - stretch) + 1


def forward_route(distance, cycle):
    total = 2 * cycle
    return [
        (stretch_device(s, cycle), stretch_device((s + distance) % total, cycle))
        for s in range(total)
    ]


def rotary_tables(stretches, span, length, width):
    half = width // 2
    frequency = ROPE_BASE ** (-2.0 * np.arange(half, dtype=np.float64) / width)
    before = np.maximum(np.arange(stretches)[:, None] - np.arange(span + 1), 0).astype(np.float64)
    base = (before * length)[:, :, None] * frequency
    offset = np.arange(length, dtype=np.float64)[:, None] * frequency
    base = np.concatenate([np.cos(base), np.sin(base)], axis=-1)
    offset = np.concatenate([np.cos(offset), np.sin(offset)], axis=-1)
    return base.astype(np.float32), offset.astype(np.float32)


def my_stretch(cycle):
    block = lax.axis_index("blk")
    return jnp.where(lax.axis_index("uly") == 0, block, 2 * cycle - 1 - block)


def spread(packed):
    half = packed.shape[-1] // 2
    first = lax.broadcasted_iota(jnp.int32, packed.shape, 1) < half
    turned = pltpu.roll(packed, half, 1)
    return jnp.where(first, packed, turned), jnp.where(first, turned, packed)


def gained_tables(base, offset, gain):
    width = gain.shape[-1]
    half = width // 2
    gain = gain * math.sqrt(width)
    turned_gain = pltpu.roll(gain, half, 1)
    turned_gain = jnp.where(lax.broadcasted_iota(jnp.int32, gain.shape, 1) < half, -turned_gain, turned_gain)
    (base_cos, base_sin), (cosine, sine) = base, offset
    return gain * (base_cos * cosine - base_sin * sine), turned_gain * (base_sin * cosine + base_cos * sine)


def half_turn(width):
    rows = lax.broadcasted_iota(jnp.int32, (width, width), 0)
    columns = lax.broadcasted_iota(jnp.int32, (width, width), 1)
    swapped = jnp.where(columns < width // 2, columns + width // 2, columns - width // 2)
    return (rows == swapped).astype(jnp.float32).astype(jnp.bfloat16)


def rotate_head(raw, cosine, sine, swap):
    values = raw.astype(jnp.float32)
    width = values.shape[-1]
    square_sum = jnp.sum(values * values, axis=-1, keepdims=True)
    turned = values * cosine + matmul(raw, swap) * sine
    return (turned * lax.rsqrt(square_sum + width * EPSILON)).astype(jnp.bfloat16)


def columns_of(block, width):
    if isinstance(block, int):
        return slice(block * width, (block + 1) * width)
    return pl.ds(pl.multiple_of(block * width, width), width)


def loop(rolled, count, body):
    if rolled:
        lax.fori_loop(0, count, body, None)
    else:
        for g in range(count):
            body(g, None)


def matmul(left, right):
    return jnp.dot(left, right, preferred_element_type=jnp.float32)


def matmul_t(left, right):
    return lax.dot_general(left, right, (((1,), (1,)), ((), ())), preferred_element_type=jnp.float32)


def pair_positions(length):
    shape = (length, PAIR * length)
    columns = lax.broadcasted_iota(jnp.int32, shape, 1)
    return lax.broadcasted_iota(jnp.int32, shape, 0), lax.rem(columns, length)


def put_pair(stage_ref, g, n, mixed):
    width = mixed.shape[0]
    turned = mixed.T
    length = turned.shape[0] // PAIR
    for i in range(PAIR):
        stage_ref[g, :, columns_of(n * PAIR + i, width)] = turned[i * length : (i + 1) * length]


def start_store(stage_ref, out_hbm, out_sem, g):
    place = columns_of(g, stage_ref.shape[2])
    pltpu.make_async_copy(stage_ref.at[g], out_hbm.at[:, place], out_sem).start()


def wait_stores(stage_ref, out_sem):
    pltpu.make_async_copy(stage_ref, stage_ref, out_sem).wait()


def local_kernel(
    cycle,
    span,
    q_hbm,
    k_hbm,
    v_hbm,
    q_gain_hbm,
    k_gain_hbm,
    base_hbm,
    offset_hbm,
    rotated_ref,
    score_ref,
    table_ref,
    value_ref,
    out_hbm,
    q_ref,
    k_ref,
    q_gain_ref,
    k_gain_ref,
    base_ref,
    offset_ref,
    small_sem,
    q_sem,
    v_sem,
    stage_ref,
    out_sem,
):
    heads, length, width = rotated_ref.shape
    kv_heads = k_ref.shape[1] // width
    group = heads // kv_heads
    stretch = my_stretch(cycle)
    smalls = [
        pltpu.make_async_copy(source, target, small_sem.at[i])
        for i, (source, target) in enumerate(
            [
                (q_gain_hbm, q_gain_ref),
                (k_gain_hbm, k_gain_ref),
                (base_hbm.at[stretch], base_ref),
                (offset_hbm, offset_ref),
                (k_hbm, k_ref),
            ]
        )
    ]
    for copy in smalls:
        copy.start()

    def q_copy(g):
        return pltpu.make_async_copy(q_hbm.at[:, columns_of(g, group * width)], q_ref.at[g], q_sem.at[g])

    for g in range(kv_heads):
        q_copy(g).start()
    v_copy = pltpu.make_async_copy(v_hbm, value_ref, v_sem)
    v_copy.start()
    for copy in smalls:
        copy.wait()

    k_gain = k_gain_ref[...]
    bases = [spread(base_ref[d : d + 1]) for d in range(span + 1)]
    offset = spread(offset_ref[...])
    q_cos, q_sin = gained_tables(bases[0], offset, q_gain_ref[...])
    k_cos, k_sin = gained_tables(bases[0], offset, k_gain)
    for d in range(span):
        table_ref[d, 0], table_ref[d, 1] = gained_tables(bases[d + 1], offset, k_gain)
    swap = half_turn(width)
    keys = [rotate_head(k_ref[:, columns_of(g, width)], k_cos, k_sin, swap) for g in range(kv_heads)]

    def score(g):
        for n in range(g * group // PAIR, (g + 1) * group // PAIR):
            queries = rotated_ref[n * PAIR : (n + 1) * PAIR].reshape(PAIR * length, width)
            score_ref[n] = matmul_t(keys[g], queries)

    first = 0
    for count in [2, 2]:
        some = range(first, first + count)
        for g in some:
            q_copy(g).wait()
        for g in some:
            for i in range(group):
                rotated_ref[g * group + i] = rotate_head(q_ref[g, :, i * width : (i + 1) * width], q_cos, q_sin, swap)
        for g in range(max(first - 1, 0), first + count - 1):
            score(g)
        first += count
    score(kv_heads - 1)
    v_copy.wait()

    @pl.when(stretch == 0)
    def _():
        keys_at, queries_at = pair_positions(length)
        own = keys_at <= queries_at
        to_exponent = math.log2(math.e) / math.sqrt(width)
        for g in range(kv_heads):
            values = value_ref[:, columns_of(g, width)].T
            for n in range(group // PAIR):
                tile = jnp.where(own, score_ref[g * group // PAIR + n], NEG_FILL)
                weights = jnp.exp2((tile - jnp.max(tile, axis=0, keepdims=True)) * to_exponent)
                inverse = 1.0 / jnp.sum(weights, axis=0, keepdims=True)
                mixed = matmul(values, weights.astype(jnp.bfloat16))
                put_pair(stage_ref, g, n, (mixed * inverse).astype(jnp.bfloat16))
            start_store(stage_ref, out_hbm, out_sem, g)
        wait_stores(stage_ref, out_sem)


def weight_kernel(cycle, span, *refs):
    @pl.when(my_stretch(cycle) > 0)
    def _():
        later_weights(cycle, span, *refs)


def later_weights(cycle, span, rotated_ref, score_ref, table_ref, *refs):
    key_refs = refs[:span]
    weight_ref, inverse_ref = refs[span:]
    heads, length, width = rotated_ref.shape
    kv_heads = key_refs[0].shape[1] // width
    group = heads // kv_heads
    stretch = my_stretch(cycle)
    swap = half_turn(width)
    to_exponent = math.log2(math.e) / math.sqrt(width)
    keys_at, queries_at = pair_positions(length)
    own = keys_at <= queries_at
    keys = [
        [
            rotate_head(key_refs[d][:, columns_of(g, width)], table_ref[d, 0], table_ref[d, 1], swap)
            for d in range(span)
        ]
        for g in range(kv_heads)
    ]
    for n in range(heads // PAIR):
        queries = rotated_ref[n * PAIR : (n + 1) * PAIR].reshape(PAIR * length, width)
        far = [matmul_t(key, queries) for key in keys[n * PAIR // group]]
        last = far[span - 1]
        if span > 1:
            last = jnp.where(stretch >= span, last, NEG_FILL)
        tiles = [jnp.where(own, score_ref[n], last)]
        for d in range(span - 1):
            tiles.append(jnp.where(stretch > d, far[d], NEG_FILL))
        top = jnp.max(functools.reduce(jnp.maximum, tiles), axis=0, keepdims=True)
        weights = [jnp.exp2((tile - top) * to_exponent) for tile in tiles]
        inverse_ref[n] = 1.0 / jnp.sum(functools.reduce(jnp.add, weights), axis=0, keepdims=True)
        weights = [jnp.where(own, weights[0], 0.0), *weights[1:], jnp.where(own, 0.0, weights[0])]
        for d in range(span + 1):
            weight_ref[n, d * length : (d + 1) * length] = weights[d].astype(jnp.bfloat16)


def mix_kernel(cycle, weight_ref, inverse_ref, *refs):
    out_hbm, stage_ref, out_sem = refs[-3:]
    value_refs = refs[:-4]
    pairs, keys, _ = weight_ref.shape
    kv_heads, length, group_width = stage_ref.shape
    group_pairs = pairs // kv_heads
    width = group_width // group_pairs // PAIR

    @pl.when(my_stretch(cycle) > 0)
    def _():
        for g in range(kv_heads):
            values = jnp.concatenate([ref[:, columns_of(g, width)].T for ref in value_refs], axis=1)
            for n in range(group_pairs):
                mixed = matmul(values, weight_ref[g * group_pairs + n]) * inverse_ref[g * group_pairs + n]
                put_pair(stage_ref, g, n, mixed.astype(jnp.bfloat16))
            start_store(stage_ref, out_hbm, out_sem, g)
        wait_stores(stage_ref, out_sem)


def local(query_proj, key_proj, value_projection, query_gain, key_gain):
    cycle = lax.axis_size("blk")
    span = max(1, cycle // 64)
    length, query_width = query_proj.shape
    kv_width = key_proj.shape[1]
    width = query_gain.shape[0]
    heads = query_width // width
    kv_heads = kv_width // width
    params = pltpu.CompilerParams(vmem_limit_bytes=VMEM_LIMIT)
    vmem = pl.BlockSpec(memory_space=pltpu.VMEM)
    hbm = pl.BlockSpec(memory_space=pltpu.HBM)

    routes = [forward_route(d, cycle) for d in range(1, span + 1)]
    far_keys = [lax.ppermute(key_proj, ("blk", "uly"), route) for route in routes]
    far_values = [lax.ppermute(value_projection, ("blk", "uly"), route) for route in routes]

    base, offset = rotary_tables(2 * cycle, span, length, width)
    operands = (query_proj, key_proj, value_projection, query_gain[None], key_gain[None], base, offset)
    rotated, scores, tables, values, out = pl.pallas_call(
        functools.partial(local_kernel, cycle, span),
        in_specs=[hbm] * 7,
        out_specs=[vmem] * 4 + [hbm],
        out_shape=[
            pltpu.VMEM((heads, length, width), jnp.bfloat16),
            pltpu.VMEM((heads // PAIR, length, PAIR * length), jnp.float32),
            pltpu.VMEM((span, 2, length, width), jnp.float32),
            pltpu.VMEM((length, kv_width), jnp.bfloat16),
            jax.ShapeDtypeStruct(query_proj.shape, jnp.bfloat16),
        ],
        scratch_shapes=[
            pltpu.VMEM((kv_heads, length, query_width // kv_heads), jnp.bfloat16),
            pltpu.VMEM((length, kv_width), jnp.bfloat16),
            pltpu.VMEM((1, width), jnp.float32),
            pltpu.VMEM((1, width), jnp.float32),
            pltpu.VMEM(base.shape[1:], jnp.float32),
            pltpu.VMEM(offset.shape, jnp.float32),
            pltpu.SemaphoreType.DMA((5,)),
            pltpu.SemaphoreType.DMA((kv_heads,)),
            pltpu.SemaphoreType.DMA,
            pltpu.VMEM((kv_heads, length, query_width // kv_heads), jnp.bfloat16),
            pltpu.SemaphoreType.DMA,
        ],
        compiler_params=params,
        name="local_scores",
    )(*[pltpu.with_memory_space_constraint(x, pltpu.HBM) for x in operands])
    weights, inverse = pl.pallas_call(
        functools.partial(weight_kernel, cycle, span),
        in_specs=[vmem] * (3 + span),
        out_specs=[vmem] * 2,
        out_shape=[
            pltpu.VMEM((heads // PAIR, (span + 1) * length, PAIR * length), jnp.bfloat16),
            pltpu.VMEM((heads // PAIR, 1, PAIR * length), jnp.float32),
        ],
        compiler_params=params,
        name="weights",
    )(rotated, scores, tables, *far_keys)
    return pl.pallas_call(
        functools.partial(mix_kernel, cycle),
        in_specs=[vmem] * (3 + span) + [hbm],
        out_specs=hbm,
        out_shape=jax.ShapeDtypeStruct(query_proj.shape, jnp.bfloat16),
        input_output_aliases={3 + span: 0},
        scratch_shapes=[
            pltpu.VMEM((kv_heads, length, query_width // kv_heads), jnp.bfloat16),
            pltpu.SemaphoreType.DMA,
        ],
        compiler_params=params,
        name="mix_values",
    )(weights, inverse, values, *far_values, out)


def solution(mesh):
    placed = P(("groups", "blk", "uly"), None)
    return jax.shard_map(
        local,
        mesh=mesh,
        in_specs=(placed, placed, placed, P(), P()),
        out_specs=placed,
        check_vma=False,
    )
```

```python
import functools
import math

import jax
import jax.numpy as jnp
import numpy as np
from jax import lax
from jax.experimental import pallas as pl
from jax.experimental.pallas import tpu as pltpu
from jax.sharding import PartitionSpec as P

NEG_FILL = -1e30
ROPE_BASE = 1000000.0
EPSILON = 1e-06
PAIR = 2
DOT_PAIRS = 1
LAG, MIX_LAG, MIX_PAIRS, KEY_AHEAD = 1, 2, 2, 16
LOOP_A, LOOP_B, LOOP_C = False, False, False
VMEM_LIMIT = 16 * 1024 * 1024


def stretch_device(stretch, cycle):
    return 2 * stretch if stretch < cycle else 2 * (2 * cycle - 1 - stretch) + 1


def forward_route(distance, cycle):
    total = 2 * cycle
    return [
        (stretch_device(s, cycle), stretch_device((s + distance) % total, cycle))
        for s in range(total)
    ]


def rotary_tables(stretches, span, length, width):
    half = width // 2
    frequency = ROPE_BASE ** (-2.0 * np.arange(half, dtype=np.float64) / width)
    before = np.maximum(np.arange(stretches)[:, None] - np.arange(span + 1), 0).astype(np.float64)
    base = (before * length)[:, :, None] * frequency
    offset = np.arange(length, dtype=np.float64)[:, None] * frequency
    base = np.concatenate([np.cos(base), np.sin(base)], axis=-1)
    offset = np.concatenate([np.cos(offset), np.sin(offset)], axis=-1)
    return base.astype(np.float32), offset.astype(np.float32)


def my_stretch(cycle):
    block = lax.axis_index("blk")
    return jnp.where(lax.axis_index("uly") == 0, block, 2 * cycle - 1 - block)


def spread(packed):
    half = packed.shape[-1] // 2
    first = lax.broadcasted_iota(jnp.int32, packed.shape, 1) < half
    turned = pltpu.roll(packed, half, 1)
    return jnp.where(first, packed, turned), jnp.where(first, turned, packed)


def gained_tables(base, offset, gain):
    width = gain.shape[-1]
    half = width // 2
    gain = gain * math.sqrt(width)
    turned_gain = pltpu.roll(gain, half, 1)
    turned_gain = jnp.where(lax.broadcasted_iota(jnp.int32, gain.shape, 1) < half, -turned_gain, turned_gain)
    (base_cos, base_sin), (cosine, sine) = base, offset
    return gain * (base_cos * cosine - base_sin * sine), turned_gain * (base_sin * cosine + base_cos * sine)


def half_turn(width):
    rows = lax.broadcasted_iota(jnp.int32, (width, width), 0)
    columns = lax.broadcasted_iota(jnp.int32, (width, width), 1)
    swapped = jnp.where(columns < width // 2, columns + width // 2, columns - width // 2)
    return (rows == swapped).astype(jnp.float32).astype(jnp.bfloat16)


def rotate_head(raw, cosine, sine, swap):
    values = raw.astype(jnp.float32)
    width = values.shape[-1]
    square_sum = jnp.sum(values * values, axis=-1, keepdims=True)
    turned = values * cosine + matmul(raw, swap) * sine
    return (turned * lax.rsqrt(square_sum + width * EPSILON)).astype(jnp.bfloat16)


def columns_of(block, width):
    if isinstance(block, int):
        return slice(block * width, (block + 1) * width)
    return pl.ds(pl.multiple_of(block * width, width), width)


def loop(rolled, count, body):
    if rolled:
        lax.fori_loop(0, count, body, None)
    else:
        for g in range(count):
            body(g, None)


def matmul(left, right):
    return jnp.dot(left, right, preferred_element_type=jnp.float32)


def matmul_t(left, right):
    return lax.dot_general(left, right, (((1,), (1,)), ((), ())), preferred_element_type=jnp.float32)


def pair_positions(length):
    shape = (length, PAIR * length)
    columns = lax.broadcasted_iota(jnp.int32, shape, 1)
    return lax.broadcasted_iota(jnp.int32, shape, 0), lax.rem(columns, length)


def put_pair(stage_ref, g, n, mixed):
    width = mixed.shape[0]
    turned = mixed.T
    length = turned.shape[0] // PAIR
    for i in range(PAIR):
        stage_ref[g, :, columns_of(n * PAIR + i, width)] = turned[i * length : (i + 1) * length]


def start_store(stage_ref, out_hbm, out_sem, g):
    place = columns_of(g, stage_ref.shape[2])
    pltpu.make_async_copy(stage_ref.at[g], out_hbm.at[:, place], out_sem).start()


def wait_stores(stage_ref, out_sem):
    pltpu.make_async_copy(stage_ref, stage_ref, out_sem).wait()


def local_kernel(
    cycle,
    span,
    q_hbm,
    k_hbm,
    v_hbm,
    q_gain_hbm,
    k_gain_hbm,
    base_hbm,
    offset_hbm,
    rotated_ref,
    score_ref,
    table_ref,
    value_ref,
    out_hbm,
    q_ref,
    k_ref,
    q_gain_ref,
    k_gain_ref,
    base_ref,
    offset_ref,
    small_sem,
    q_sem,
    v_sem,
    stage_ref,
    out_sem,
):
    heads, length, width = rotated_ref.shape
    kv_heads = k_ref.shape[1] // width
    group = heads // kv_heads
    stretch = my_stretch(cycle)
    smalls = [
        pltpu.make_async_copy(source, target, small_sem.at[i])
        for i, (source, target) in enumerate(
            [
                (q_gain_hbm, q_gain_ref),
                (k_gain_hbm, k_gain_ref),
                (base_hbm.at[stretch], base_ref),
                (offset_hbm, offset_ref),
                (k_hbm, k_ref),
            ]
        )
    ]
    for copy in smalls:
        copy.start()

    def q_copy(g):
        return pltpu.make_async_copy(q_hbm.at[:, columns_of(g, group * width)], q_ref.at[g], q_sem.at[g])

    for g in range(kv_heads):
        q_copy(g).start()
    v_copy = pltpu.make_async_copy(v_hbm, value_ref, v_sem)
    v_copy.start()
    for copy in smalls:
        copy.wait()

    k_gain = k_gain_ref[...]
    bases = [spread(base_ref[d : d + 1]) for d in range(span + 1)]
    offset = spread(offset_ref[...])
    q_cos, q_sin = gained_tables(bases[0], offset, q_gain_ref[...])
    k_cos, k_sin = gained_tables(bases[0], offset, k_gain)
    for d in range(span):
        table_ref[d, 0], table_ref[d, 1] = gained_tables(bases[d + 1], offset, k_gain)
    swap = half_turn(width)
    keys = [rotate_head(k_ref[:, columns_of(g, width)], k_cos, k_sin, swap) for g in range(kv_heads)]

    def score(g):
        for n in range(g * group // PAIR, (g + 1) * group // PAIR):
            queries = rotated_ref[n * PAIR : (n + 1) * PAIR].reshape(PAIR * length, width)
            score_ref[n] = matmul_t(keys[g], queries)

    first = 0
    for count in [2, 2]:
        some = range(first, first + count)
        for g in some:
            q_copy(g).wait()
        for g in some:
            for i in range(group):
                rotated_ref[g * group + i] = rotate_head(q_ref[g, :, i * width : (i + 1) * width], q_cos, q_sin, swap)
        for g in range(max(first - 1, 0), first + count - 1):
            score(g)
        first += count
    score(kv_heads - 1)
    v_copy.wait()

    @pl.when(stretch == 0)
    def _():
        keys_at, queries_at = pair_positions(length)
        own = keys_at <= queries_at
        to_exponent = math.log2(math.e) / math.sqrt(width)
        for g in range(kv_heads):
            values = value_ref[:, columns_of(g, width)].T
            for n in range(group // PAIR):
                tile = jnp.where(own, score_ref[g * group // PAIR + n], NEG_FILL)
                weights = jnp.exp2((tile - jnp.max(tile, axis=0, keepdims=True)) * to_exponent)
                inverse = 1.0 / jnp.sum(weights, axis=0, keepdims=True)
                mixed = matmul(values, weights.astype(jnp.bfloat16))
                put_pair(stage_ref, g, n, (mixed * inverse).astype(jnp.bfloat16))
            start_store(stage_ref, out_hbm, out_sem, g)
        wait_stores(stage_ref, out_sem)


def weight_kernel(cycle, span, *refs):
    @pl.when(my_stretch(cycle) > 0)
    def _():
        later_weights(cycle, span, *refs)


def later_weights(cycle, span, rotated_ref, score_ref, table_ref, value_ref, *refs):
    key_refs = refs[:span]
    weight_ref, mixed_ref, near_ref = refs[span:]
    heads, length, width = rotated_ref.shape
    pairs = heads // PAIR
    kv_heads = key_refs[0].shape[1] // width
    group_pairs = pairs // kv_heads
    stretch = my_stretch(cycle)
    swap = half_turn(width)
    to_exponent = math.log2(math.e) / math.sqrt(width)
    rows = lax.broadcasted_iota(jnp.int32, (length, length), 0)
    columns = lax.broadcasted_iota(jnp.int32, (length, length), 1)
    own = rows <= columns
    near_part = (columns <= rows).astype(jnp.float32).astype(jnp.bfloat16)
    near_part = jnp.concatenate([near_part] * PAIR, axis=0)
    keys = []

    def rotate_keys(g):
        keys.append(
            [
                rotate_head(key_refs[d][:, columns_of(g, width)], table_ref[d, 0], table_ref[d, 1], swap)
                for d in range(span)
            ]
        )

    def weigh(n):
        queries = rotated_ref[n * PAIR : (n + 1) * PAIR].reshape(PAIR * length, width)
        tiles = [matmul_t(key, queries) for key in keys[n // group_pairs]]
        if span > 1:
            tiles = [jnp.where(stretch > d, tiles[d], NEG_FILL) for d in range(span)]
        merged = []
        for i in range(PAIR):
            place = columns_of(i, length)
            merged.append(jnp.where(own, score_ref[n, :, place], tiles[span - 1][:, place]))
        tiles[span - 1] = jnp.concatenate(merged, axis=1)
        top = jnp.max(functools.reduce(jnp.maximum, tiles), axis=0, keepdims=True)
        weights = [jnp.exp2((tile - top) * to_exponent) for tile in tiles]
        inverse = 1.0 / jnp.sum(functools.reduce(jnp.add, weights), axis=0, keepdims=True)
        return [(w * inverse).astype(jnp.bfloat16) for w in weights]

    def put(n, weights):
        for d in range(span):
            turned = weights[d].T
            if d == span - 1:
                near = turned * near_part
                near_ref[n] = near
                turned = turned - near
            weight_ref[n, :, d * length : (d + 1) * length] = turned

    def mix_near(first):
        some = slice(first, first + MIX_PAIRS)
        near = near_ref[some].reshape(MIX_PAIRS * PAIR * length, length)
        mixed = matmul(near, value_ref[:, columns_of(first // group_pairs, width)])
        mixed_ref[some] = mixed.reshape(MIX_PAIRS, PAIR * length, width)

    held = []
    for n in range(pairs + max(LAG, MIX_LAG)):
        while len(keys) < min(kv_heads, (n + KEY_AHEAD) // group_pairs + 1):
            rotate_keys(len(keys))
        if n < pairs:
            held.append((n, weigh(n)))
        if n >= LAG and held:
            put(*held.pop(0))
        mixed = n + 1 - MIX_LAG
        if 0 < mixed <= pairs and mixed % MIX_PAIRS == 0:
            mix_near(mixed - MIX_PAIRS)


def mix_kernel(cycle, weight_ref, mixed_ref, *refs):
    out_hbm, stage_ref, out_sem = refs[-3:]
    value_refs = refs[:-4]
    pairs, rows, keys = weight_ref.shape
    kv_heads, length, group_width = stage_ref.shape
    group_pairs = pairs // kv_heads
    width = group_width // group_pairs // PAIR

    @pl.when(my_stretch(cycle) > 0)
    def _():
        for g in range(kv_heads):
            values = jnp.concatenate([ref[:, columns_of(g, width)] for ref in value_refs], axis=0)
            for first in range(0, group_pairs, DOT_PAIRS):
                some = slice(g * group_pairs + first, g * group_pairs + first + DOT_PAIRS)
                mixed = matmul(weight_ref[some].reshape(DOT_PAIRS * rows, keys), values)
                mixed = mixed + mixed_ref[some].reshape(DOT_PAIRS * rows, width)
                for i in range(DOT_PAIRS * PAIR):
                    part = mixed[i * length : (i + 1) * length].astype(jnp.bfloat16)
                    stage_ref[g, :, columns_of(first * PAIR + i, width)] = part
            start_store(stage_ref, out_hbm, out_sem, g)
        wait_stores(stage_ref, out_sem)


def local(query_proj, key_proj, value_projection, query_gain, key_gain):
    cycle = lax.axis_size("blk")
    span = max(1, cycle // 64)
    length, query_width = query_proj.shape
    kv_width = key_proj.shape[1]
    width = query_gain.shape[0]
    heads = query_width // width
    kv_heads = kv_width // width
    params = pltpu.CompilerParams(vmem_limit_bytes=VMEM_LIMIT)
    vmem = pl.BlockSpec(memory_space=pltpu.VMEM)
    hbm = pl.BlockSpec(memory_space=pltpu.HBM)

    routes = [forward_route(d, cycle) for d in range(1, span + 1)]
    far_keys = [lax.ppermute(key_proj, ("blk", "uly"), route) for route in routes]

    def copy_kernel(source, target, sem):
        copy = pltpu.make_async_copy(source, target, sem)
        copy.start()
        copy.wait()

    v_copied = pl.pallas_call(
        copy_kernel,
        in_specs=[hbm],
        out_specs=vmem,
        out_shape=pltpu.VMEM(value_projection.shape, jnp.bfloat16),
        scratch_shapes=[pltpu.SemaphoreType.DMA],
        name="copy_values",
    )(pltpu.with_memory_space_constraint(value_projection, pltpu.HBM))
    far_values = [lax.ppermute(v_copied, ("blk", "uly"), route) for route in routes]

    base, offset = rotary_tables(2 * cycle, span, length, width)
    operands = (query_proj, key_proj, value_projection, query_gain[None], key_gain[None], base, offset)
    rotated, scores, tables, values, out = pl.pallas_call(
        functools.partial(local_kernel, cycle, span),
        in_specs=[hbm] * 7,
        out_specs=[vmem] * 4 + [hbm],
        out_shape=[
            pltpu.VMEM((heads, length, width), jnp.bfloat16),
            pltpu.VMEM((heads // PAIR, length, PAIR * length), jnp.float32),
            pltpu.VMEM((span, 2, length, width), jnp.float32),
            pltpu.VMEM((length, kv_width), jnp.bfloat16),
            jax.ShapeDtypeStruct(query_proj.shape, jnp.bfloat16),
        ],
        scratch_shapes=[
            pltpu.VMEM((kv_heads, length, query_width // kv_heads), jnp.bfloat16),
            pltpu.VMEM((length, kv_width), jnp.bfloat16),
            pltpu.VMEM((1, width), jnp.float32),
            pltpu.VMEM((1, width), jnp.float32),
            pltpu.VMEM(base.shape[1:], jnp.float32),
            pltpu.VMEM(offset.shape, jnp.float32),
            pltpu.SemaphoreType.DMA((5,)),
            pltpu.SemaphoreType.DMA((kv_heads,)),
            pltpu.SemaphoreType.DMA,
            pltpu.VMEM((kv_heads, length, query_width // kv_heads), jnp.bfloat16),
            pltpu.SemaphoreType.DMA,
        ],
        compiler_params=params,
        name="local_scores",
    )(*[pltpu.with_memory_space_constraint(x, pltpu.HBM) for x in operands])
    partial = pl.pallas_call(
        functools.partial(weight_kernel, cycle, span),
        in_specs=[vmem] * (4 + span),
        out_specs=[vmem] * 2,
        out_shape=[
            pltpu.VMEM((heads // PAIR, PAIR * length, span * length), jnp.bfloat16),
            pltpu.VMEM((heads // PAIR, PAIR * length, width), jnp.float32),
        ],
        scratch_shapes=[pltpu.VMEM((heads // PAIR, PAIR * length, length), jnp.bfloat16)],
        compiler_params=params,
        name="weights",
    )(rotated, scores, tables, values, *far_keys)
    return pl.pallas_call(
        functools.partial(mix_kernel, cycle),
        in_specs=[vmem] * (2 + span) + [hbm],
        out_specs=hbm,
        out_shape=jax.ShapeDtypeStruct(query_proj.shape, jnp.bfloat16),
        input_output_aliases={2 + span: 0},
        scratch_shapes=[
            pltpu.VMEM((kv_heads, length, query_width // kv_heads), jnp.bfloat16),
            pltpu.SemaphoreType.DMA,
        ],
        compiler_params=params,
        name="mix_values",
    )(*partial, *far_values, out)


def solution(mesh):
    placed = P(("groups", "blk", "uly"), None)
    return jax.shard_map(
        local,
        mesh=mesh,
        in_specs=(placed, placed, placed, P(), P()),
        out_specs=placed,
        check_vma=False,
    )
```

```python
import functools
import math

import jax
import jax.numpy as jnp
import numpy as np
from jax import lax
from jax.experimental import pallas as pl
from jax.experimental.pallas import tpu as pltpu
from jax.sharding import PartitionSpec as P

NEG_FILL = -1e30
ROPE_BASE = 1000000.0
EPSILON = 1e-06
PAIR = 2
LAG = 1
STORE_AFTER = (0, 2, 5, 8, 11, 13)
VMEM_LIMIT = 16 * 1024 * 1024


def stretch_device(stretch, cycle):
    return 2 * stretch if stretch < cycle else 2 * (2 * cycle - 1 - stretch) + 1


def forward_route(distance, cycle):
    total = 2 * cycle
    return [
        (stretch_device(s, cycle), stretch_device((s + distance) % total, cycle))
        for s in range(total)
    ]


def rotary_tables(stretches, span, length, width):
    half = width // 2
    frequency = ROPE_BASE ** (-2.0 * np.arange(half, dtype=np.float64) / width)
    before = np.maximum(np.arange(stretches)[:, None] - np.arange(span + 1), 0).astype(np.float64)
    base = (before * length)[:, :, None] * frequency
    offset = np.arange(length, dtype=np.float64)[:, None] * frequency
    base = np.concatenate([np.cos(base), np.sin(base)], axis=-1)
    offset = np.concatenate([np.cos(offset), np.sin(offset)], axis=-1)
    return base.astype(np.float32), offset.astype(np.float32)


def my_stretch(cycle):
    block = lax.axis_index("blk")
    return jnp.where(lax.axis_index("uly") == 0, block, 2 * cycle - 1 - block)


def spread(packed):
    half = packed.shape[-1] // 2
    first = lax.broadcasted_iota(jnp.int32, packed.shape, 1) < half
    turned = pltpu.roll(packed, half, 1)
    return jnp.where(first, packed, turned), jnp.where(first, turned, packed)


def gained_tables(base, offset, gain):
    width = gain.shape[-1]
    half = width // 2
    gain = gain * math.sqrt(width)
    turned_gain = pltpu.roll(gain, half, 1)
    turned_gain = jnp.where(lax.broadcasted_iota(jnp.int32, gain.shape, 1) < half, -turned_gain, turned_gain)
    (base_cos, base_sin), (cosine, sine) = base, offset
    return gain * (base_cos * cosine - base_sin * sine), turned_gain * (base_sin * cosine + base_cos * sine)


def half_turn(width):
    rows = lax.broadcasted_iota(jnp.int32, (width, width), 0)
    columns = lax.broadcasted_iota(jnp.int32, (width, width), 1)
    swapped = jnp.where(columns < width // 2, columns + width // 2, columns - width // 2)
    return (rows == swapped).astype(jnp.float32).astype(jnp.bfloat16)


def rotate_head(raw, cosine, sine, swap):
    values = raw.astype(jnp.float32)
    width = values.shape[-1]
    square_sum = jnp.sum(values * values, axis=-1, keepdims=True)
    turned = values * cosine + matmul(raw, swap) * sine
    return (turned * lax.rsqrt(square_sum + width * EPSILON)).astype(jnp.bfloat16)


def columns_of(block, width):
    if isinstance(block, int):
        return slice(block * width, (block + 1) * width)
    return pl.ds(pl.multiple_of(block * width, width), width)


def matmul(left, right):
    return jnp.dot(left, right, preferred_element_type=jnp.float32)


def matmul_t(left, right):
    return lax.dot_general(left, right, (((1,), (1,)), ((), ())), preferred_element_type=jnp.float32)


def pair_positions(length):
    shape = (length, PAIR * length)
    columns = lax.broadcasted_iota(jnp.int32, shape, 1)
    return lax.broadcasted_iota(jnp.int32, shape, 0), lax.rem(columns, length)


def put_pair(stage_ref, g, n, mixed):
    width = mixed.shape[0]
    turned = mixed.T
    length = turned.shape[0] // PAIR
    for i in range(PAIR):
        stage_ref[g, :, columns_of(n * PAIR + i, width)] = turned[i * length : (i + 1) * length]


def start_store(stage_ref, out_hbm, out_sem, g):
    place = columns_of(g, stage_ref.shape[2])
    pltpu.make_async_copy(stage_ref.at[g], out_hbm.at[:, place], out_sem).start()


def wait_stores(stage_ref, out_sem):
    pltpu.make_async_copy(stage_ref, stage_ref, out_sem).wait()


def local_kernel(
    cycle,
    span,
    q_hbm,
    k_hbm,
    v_hbm,
    q_gain_hbm,
    k_gain_hbm,
    base_hbm,
    offset_hbm,
    rotated_ref,
    score_ref,
    table_ref,
    value_ref,
    out_hbm,
    q_ref,
    k_ref,
    v_ref,
    q_gain_ref,
    k_gain_ref,
    base_ref,
    offset_ref,
    small_sem,
    q_sem,
    v_sem,
    stage_ref,
    out_sem,
):
    heads, length, width = rotated_ref.shape
    kv_heads = k_ref.shape[1] // width
    group = heads // kv_heads
    stretch = my_stretch(cycle)
    smalls = [
        pltpu.make_async_copy(source, target, small_sem.at[i])
        for i, (source, target) in enumerate(
            [
                (q_gain_hbm, q_gain_ref),
                (k_gain_hbm, k_gain_ref),
                (base_hbm.at[stretch], base_ref),
                (offset_hbm, offset_ref),
                (k_hbm, k_ref),
            ]
        )
    ]
    for copy in smalls:
        copy.start()

    def q_copy(g):
        return pltpu.make_async_copy(q_hbm.at[:, columns_of(g, group * width)], q_ref.at[g], q_sem.at[g])

    for g in range(kv_heads):
        q_copy(g).start()
    v_copy = pltpu.make_async_copy(v_hbm, v_ref, v_sem)
    v_copy.start()
    for copy in smalls:
        copy.wait()

    k_gain = k_gain_ref[...]
    bases = [spread(base_ref[d : d + 1]) for d in range(span + 1)]
    offset = spread(offset_ref[...])
    q_cos, q_sin = gained_tables(bases[0], offset, q_gain_ref[...])
    k_cos, k_sin = gained_tables(bases[0], offset, k_gain)
    for d in range(span):
        table_ref[d, 0], table_ref[d, 1] = gained_tables(bases[d + 1], offset, k_gain)
    swap = half_turn(width)
    keys = [rotate_head(k_ref[:, columns_of(g, width)], k_cos, k_sin, swap) for g in range(kv_heads)]

    def score(g):
        for n in range(g * group // PAIR, (g + 1) * group // PAIR):
            queries = rotated_ref[n * PAIR : (n + 1) * PAIR].reshape(PAIR * length, width)
            score_ref[n] = matmul_t(keys[g], queries)

    first = 0
    for count in [2, 2]:
        some = range(first, first + count)
        for g in some:
            q_copy(g).wait()
        for g in some:
            for i in range(group):
                rotated_ref[g * group + i] = rotate_head(q_ref[g, :, i * width : (i + 1) * width], q_cos, q_sin, swap)
        for g in range(max(first - 1, 0), first + count - 1):
            score(g)
        first += count
    score(kv_heads - 1)
    v_copy.wait()
    for g in range(kv_heads):
        value_ref[g] = v_ref[:, columns_of(g, width)].T

    @pl.when(stretch == 0)
    def _():
        keys_at, queries_at = pair_positions(length)
        own = keys_at <= queries_at
        to_exponent = math.log2(math.e) / math.sqrt(width)
        for g in range(kv_heads):
            for n in range(group // PAIR):
                tile = jnp.where(own, score_ref[g * group // PAIR + n], NEG_FILL)
                weights = jnp.exp2((tile - jnp.max(tile, axis=0, keepdims=True)) * to_exponent)
                inverse = 1.0 / jnp.sum(weights, axis=0, keepdims=True)
                mixed = matmul(value_ref[g], weights.astype(jnp.bfloat16))
                put_pair(stage_ref, g, n, (mixed * inverse).astype(jnp.bfloat16))
            start_store(stage_ref, out_hbm, out_sem, g)
        wait_stores(stage_ref, out_sem)


def weight_kernel(cycle, span, *refs):
    @pl.when(my_stretch(cycle) > 0)
    def _():
        later_weights(cycle, span, *refs)


def later_weights(cycle, span, rotated_ref, score_ref, table_ref, *refs):
    key_refs = refs[:span]
    weight_ref, inverse_ref = refs[span:]
    heads, length, width = rotated_ref.shape
    kv_heads = key_refs[0].shape[1] // width
    group = heads // kv_heads
    stretch = my_stretch(cycle)
    swap = half_turn(width)
    to_exponent = math.log2(math.e) / math.sqrt(width)
    rows = lax.broadcasted_iota(jnp.int32, (length, length), 0)
    columns = lax.broadcasted_iota(jnp.int32, (length, length), 1)
    own = rows <= columns
    near_part = own.astype(jnp.float32).astype(jnp.bfloat16)
    near_part = jnp.concatenate([near_part] * PAIR, axis=1)
    keys = [
        [
            rotate_head(key_refs[d][:, columns_of(g, width)], table_ref[d, 0], table_ref[d, 1], swap)
            for d in range(span)
        ]
        for g in range(kv_heads)
    ]
    for n in range(heads // PAIR):
        queries = rotated_ref[n * PAIR : (n + 1) * PAIR].reshape(PAIR * length, width)
        far = [matmul_t(key, queries) for key in keys[n * PAIR // group]]
        if span > 1:
            far = [jnp.where(stretch > d, far[d], NEG_FILL) for d in range(span)]
        merged = []
        for i in range(PAIR):
            place = columns_of(i, length)
            merged.append(jnp.where(own, score_ref[n, :, place], far[span - 1][:, place]))
        tiles = [*far[: span - 1], jnp.concatenate(merged, axis=1)]
        top = jnp.max(functools.reduce(jnp.maximum, tiles), axis=0, keepdims=True)
        weights = [jnp.exp2((tile - top) * to_exponent) for tile in tiles]
        inverse = 1.0 / jnp.sum(functools.reduce(jnp.add, weights), axis=0, keepdims=True)
        inverse_ref[n] = inverse
        weights = [w.astype(jnp.bfloat16) for w in weights]
        near = weights[span - 1] * near_part
        weights[span - 1] = weights[span - 1] - near
        for d, part in enumerate([near, *weights]):
            weight_ref[n, d * length : (d + 1) * length] = part


def mix_kernel(cycle, weight_ref, inverse_ref, own_value_ref, *refs):
    out_hbm, stage_ref, out_sem = refs[-3:]
    value_refs = refs[:-4]
    pairs = weight_ref.shape[0]
    kv_heads, width, _ = own_value_ref.shape
    group_pairs = pairs // kv_heads

    @pl.when(my_stretch(cycle) > 0)
    def _():
        values, held, ready = [], [], []

        def mixed_pair(n):
            g = n // group_pairs
            if g == len(values):
                parts = [ref[:, columns_of(g, width)].T for ref in value_refs]
                values.append(jnp.concatenate([own_value_ref[g], *parts], axis=1))
            return (matmul(values[g], weight_ref[n]) * inverse_ref[n]).astype(jnp.bfloat16)

        def store_pair(n, mixed):
            put_pair(stage_ref, n, 0, mixed)
            ready.append(n)
            if n in STORE_AFTER or n == pairs - 1:
                for m in ready:
                    start_store(stage_ref, out_hbm, out_sem, m)
                ready.clear()

        for n in range(pairs):
            held.append((n, mixed_pair(n)))
            if len(held) > LAG:
                store_pair(*held.pop(0))
        for item in held:
            store_pair(*item)
        wait_stores(stage_ref, out_sem)


def local(query_proj, key_proj, value_projection, query_gain, key_gain):
    cycle = lax.axis_size("blk")
    span = max(1, cycle // 64)
    length, query_width = query_proj.shape
    kv_width = key_proj.shape[1]
    width = query_gain.shape[0]
    heads = query_width // width
    kv_heads = kv_width // width
    params = pltpu.CompilerParams(vmem_limit_bytes=VMEM_LIMIT)
    vmem = pl.BlockSpec(memory_space=pltpu.VMEM)
    hbm = pl.BlockSpec(memory_space=pltpu.HBM)

    routes = [forward_route(d, cycle) for d in range(1, span + 1)]
    far_keys = [lax.ppermute(key_proj, ("blk", "uly"), route) for route in routes]
    far_values = [lax.ppermute(value_projection, ("blk", "uly"), route) for route in routes]

    base, offset = rotary_tables(2 * cycle, span, length, width)
    operands = (query_proj, key_proj, value_projection, query_gain[None], key_gain[None], base, offset)
    rotated, scores, tables, values, out = pl.pallas_call(
        functools.partial(local_kernel, cycle, span),
        in_specs=[hbm] * 7,
        out_specs=[vmem] * 4 + [hbm],
        out_shape=[
            pltpu.VMEM((heads, length, width), jnp.bfloat16),
            pltpu.VMEM((heads // PAIR, length, PAIR * length), jnp.float32),
            pltpu.VMEM((span, 2, length, width), jnp.float32),
            pltpu.VMEM((kv_heads, width, length), jnp.bfloat16),
            jax.ShapeDtypeStruct(query_proj.shape, jnp.bfloat16),
        ],
        scratch_shapes=[
            pltpu.VMEM((kv_heads, length, query_width // kv_heads), jnp.bfloat16),
            pltpu.VMEM((length, kv_width), jnp.bfloat16),
            pltpu.VMEM((length, kv_width), jnp.bfloat16),
            pltpu.VMEM((1, width), jnp.float32),
            pltpu.VMEM((1, width), jnp.float32),
            pltpu.VMEM(base.shape[1:], jnp.float32),
            pltpu.VMEM(offset.shape, jnp.float32),
            pltpu.SemaphoreType.DMA((5,)),
            pltpu.SemaphoreType.DMA((kv_heads,)),
            pltpu.SemaphoreType.DMA,
            pltpu.VMEM((kv_heads, length, query_width // kv_heads), jnp.bfloat16),
            pltpu.SemaphoreType.DMA,
        ],
        compiler_params=params,
        name="local_scores",
    )(*[pltpu.with_memory_space_constraint(x, pltpu.HBM) for x in operands])
    weights, inverse = pl.pallas_call(
        functools.partial(weight_kernel, cycle, span),
        in_specs=[vmem] * (3 + span),
        out_specs=[vmem] * 2,
        out_shape=[
            pltpu.VMEM((heads // PAIR, (span + 1) * length, PAIR * length), jnp.bfloat16),
            pltpu.VMEM((heads // PAIR, 1, PAIR * length), jnp.float32),
        ],
        compiler_params=params,
        name="weights",
    )(rotated, scores, tables, *far_keys)
    return pl.pallas_call(
        functools.partial(mix_kernel, cycle),
        in_specs=[vmem] * (3 + span) + [hbm],
        out_specs=hbm,
        out_shape=jax.ShapeDtypeStruct(query_proj.shape, jnp.bfloat16),
        input_output_aliases={3 + span: 0},
        scratch_shapes=[
            pltpu.VMEM((heads // PAIR, length, PAIR * width), jnp.bfloat16),
            pltpu.SemaphoreType.DMA,
        ],
        compiler_params=params,
        name="mix_values",
    )(weights, inverse, values, *far_values, out)


def solution(mesh):
    placed = P(("groups", "blk", "uly"), None)
    return jax.shard_map(
        local,
        mesh=mesh,
        in_specs=(placed, placed, placed, P(), P()),
        out_specs=placed,
        check_vma=False,
    )
```

```python
import functools
import math

import jax
import jax.numpy as jnp
import numpy as np
from jax import lax
from jax.experimental import pallas as pl
from jax.experimental.pallas import tpu as pltpu
from jax.sharding import PartitionSpec as P

NEG_FILL = -1e30
ROPE_BASE = 1000000.0
EPSILON = 1e-06
PAIR = 2
LAG = 1
STORE_AFTER = (0, 2, 5, 8, 11, 13)
VMEM_LIMIT = 16 * 1024 * 1024


def stretch_device(stretch, cycle):
    return 2 * stretch if stretch < cycle else 2 * (2 * cycle - 1 - stretch) + 1


def forward_route(distance, cycle):
    total = 2 * cycle
    return [
        (stretch_device(s, cycle), stretch_device((s + distance) % total, cycle))
        for s in range(total)
    ]


def rotary_tables(stretches, span, length, width):
    half = width // 2
    frequency = ROPE_BASE ** (-2.0 * np.arange(half, dtype=np.float64) / width)
    before = np.maximum(np.arange(stretches)[:, None] - np.arange(span + 1), 0).astype(np.float64)
    base = (before * length)[:, :, None] * frequency
    offset = np.arange(length, dtype=np.float64)[:, None] * frequency
    base = np.concatenate([np.cos(base), np.sin(base)], axis=-1)
    offset = np.concatenate([np.cos(offset), np.sin(offset)], axis=-1)
    return base.astype(np.float32), offset.astype(np.float32)


def my_stretch(cycle):
    block = lax.axis_index("blk")
    return jnp.where(lax.axis_index("uly") == 0, block, 2 * cycle - 1 - block)


def spread(packed):
    half = packed.shape[-1] // 2
    first = lax.broadcasted_iota(jnp.int32, packed.shape, 1) < half
    turned = pltpu.roll(packed, half, 1)
    return jnp.where(first, packed, turned), jnp.where(first, turned, packed)


def gained_tables(base, offset, gain):
    width = gain.shape[-1]
    half = width // 2
    gain = gain * math.sqrt(width)
    turned_gain = pltpu.roll(gain, half, 1)
    turned_gain = jnp.where(lax.broadcasted_iota(jnp.int32, gain.shape, 1) < half, -turned_gain, turned_gain)
    (base_cos, base_sin), (cosine, sine) = base, offset
    return gain * (base_cos * cosine - base_sin * sine), turned_gain * (base_sin * cosine + base_cos * sine)


def half_turn(width):
    rows = lax.broadcasted_iota(jnp.int32, (width, width), 0)
    columns = lax.broadcasted_iota(jnp.int32, (width, width), 1)
    swapped = jnp.where(columns < width // 2, columns + width // 2, columns - width // 2)
    return (rows == swapped).astype(jnp.float32).astype(jnp.bfloat16)


def rotate_head(raw, cosine, sine, swap):
    values = raw.astype(jnp.float32)
    width = values.shape[-1]
    square_sum = jnp.sum(values * values, axis=-1, keepdims=True)
    turned = values * cosine + matmul(raw, swap) * sine
    return (turned * lax.rsqrt(square_sum + width * EPSILON)).astype(jnp.bfloat16)


def columns_of(block, width):
    if isinstance(block, int):
        return slice(block * width, (block + 1) * width)
    return pl.ds(pl.multiple_of(block * width, width), width)


def matmul(left, right):
    return jnp.dot(left, right, preferred_element_type=jnp.float32)


def matmul_t(left, right):
    return lax.dot_general(left, right, (((1,), (1,)), ((), ())), preferred_element_type=jnp.float32)


def pair_positions(length):
    shape = (length, PAIR * length)
    columns = lax.broadcasted_iota(jnp.int32, shape, 1)
    return lax.broadcasted_iota(jnp.int32, shape, 0), lax.rem(columns, length)


def put_pair(stage_ref, g, n, mixed):
    width = mixed.shape[0]
    turned = mixed.T
    length = turned.shape[0] // PAIR
    for i in range(PAIR):
        stage_ref[g, :, columns_of(n * PAIR + i, width)] = turned[i * length : (i + 1) * length]


def start_store(stage_ref, out_hbm, out_sem, g):
    place = columns_of(g, stage_ref.shape[2])
    pltpu.make_async_copy(stage_ref.at[g], out_hbm.at[:, place], out_sem).start()


def wait_stores(stage_ref, out_sem):
    pltpu.make_async_copy(stage_ref, stage_ref, out_sem).wait()


def local_kernel(
    cycle,
    span,
    q_hbm,
    k_hbm,
    v_hbm,
    q_gain_hbm,
    k_gain_hbm,
    base_hbm,
    offset_hbm,
    rotated_ref,
    score_ref,
    table_ref,
    value_ref,
    out_hbm,
    q_ref,
    k_ref,
    v_ref,
    q_gain_ref,
    k_gain_ref,
    base_ref,
    offset_ref,
    small_sem,
    q_sem,
    v_sem,
    stage_ref,
    out_sem,
):
    heads, length, width = rotated_ref.shape
    kv_heads = k_ref.shape[1] // width
    group = heads // kv_heads
    stretch = my_stretch(cycle)
    smalls = [
        pltpu.make_async_copy(source, target, small_sem.at[i])
        for i, (source, target) in enumerate(
            [
                (q_gain_hbm, q_gain_ref),
                (k_gain_hbm, k_gain_ref),
                (base_hbm.at[stretch], base_ref),
                (offset_hbm, offset_ref),
                (k_hbm, k_ref),
            ]
        )
    ]
    for copy in smalls:
        copy.start()

    def q_copy(g):
        return pltpu.make_async_copy(q_hbm.at[:, columns_of(g, group * width)], q_ref.at[g], q_sem.at[g])

    for g in range(kv_heads):
        q_copy(g).start()
    v_copy = pltpu.make_async_copy(v_hbm, v_ref, v_sem)
    v_copy.start()
    for copy in smalls:
        copy.wait()

    k_gain = k_gain_ref[...]
    bases = [spread(base_ref[d : d + 1]) for d in range(span + 1)]
    offset = spread(offset_ref[...])
    q_cos, q_sin = gained_tables(bases[0], offset, q_gain_ref[...])
    k_cos, k_sin = gained_tables(bases[0], offset, k_gain)
    for d in range(span):
        table_ref[d, 0], table_ref[d, 1] = gained_tables(bases[d + 1], offset, k_gain)
    swap = half_turn(width)
    keys = [rotate_head(k_ref[:, columns_of(g, width)], k_cos, k_sin, swap) for g in range(kv_heads)]

    def score(g):
        for n in range(g * group // PAIR, (g + 1) * group // PAIR):
            queries = rotated_ref[n * PAIR : (n + 1) * PAIR].reshape(PAIR * length, width)
            score_ref[n] = matmul_t(keys[g], queries)

    first = 0
    for count in [2, 2]:
        some = range(first, first + count)
        for g in some:
            q_copy(g).wait()
        for g in some:
            for i in range(group):
                rotated_ref[g * group + i] = rotate_head(q_ref[g, :, i * width : (i + 1) * width], q_cos, q_sin, swap)
        for g in range(max(first - 1, 0), first + count - 1):
            score(g)
        first += count
    score(kv_heads - 1)
    v_copy.wait()
    for g in range(kv_heads):
        value_ref[g] = v_ref[:, columns_of(g, width)].T

    @pl.when(stretch == 0)
    def _():
        keys_at, queries_at = pair_positions(length)
        own = keys_at <= queries_at
        to_exponent = math.log2(math.e) / math.sqrt(width)
        for g in range(kv_heads):
            for n in range(group // PAIR):
                tile = jnp.where(own, score_ref[g * group // PAIR + n], NEG_FILL)
                weights = jnp.exp2((tile - jnp.max(tile, axis=0, keepdims=True)) * to_exponent)
                inverse = 1.0 / jnp.sum(weights, axis=0, keepdims=True)
                mixed = matmul(value_ref[g], weights.astype(jnp.bfloat16))
                put_pair(stage_ref, g, n, (mixed * inverse).astype(jnp.bfloat16))
            start_store(stage_ref, out_hbm, out_sem, g)
        wait_stores(stage_ref, out_sem)


def weight_kernel(cycle, span, *refs):
    @pl.when(my_stretch(cycle) > 0)
    def _():
        later_weights(cycle, span, *refs)


def later_weights(cycle, span, rotated_ref, score_ref, table_ref, own_value_ref, *refs):
    key_refs = refs[:span]
    weight_ref, mixed_ref, inverse_ref = refs[span:]
    heads, length, width = rotated_ref.shape
    kv_heads = key_refs[0].shape[1] // width
    group = heads // kv_heads
    stretch = my_stretch(cycle)
    swap = half_turn(width)
    to_exponent = math.log2(math.e) / math.sqrt(width)
    rows = lax.broadcasted_iota(jnp.int32, (length, length), 0)
    columns = lax.broadcasted_iota(jnp.int32, (length, length), 1)
    own = rows <= columns
    near_part = own.astype(jnp.float32).astype(jnp.bfloat16)
    near_part = jnp.concatenate([near_part] * PAIR, axis=1)
    keys = [
        [
            rotate_head(key_refs[d][:, columns_of(g, width)], table_ref[d, 0], table_ref[d, 1], swap)
            for d in range(span)
        ]
        for g in range(kv_heads)
    ]
    for n in range(heads // PAIR):
        queries = rotated_ref[n * PAIR : (n + 1) * PAIR].reshape(PAIR * length, width)
        far = [matmul_t(key, queries) for key in keys[n * PAIR // group]]
        if span > 1:
            far = [jnp.where(stretch > d, far[d], NEG_FILL) for d in range(span)]
        merged = []
        for i in range(PAIR):
            place = columns_of(i, length)
            merged.append(jnp.where(own, score_ref[n, :, place], far[span - 1][:, place]))
        tiles = [*far[: span - 1], jnp.concatenate(merged, axis=1)]
        top = jnp.max(functools.reduce(jnp.maximum, tiles), axis=0, keepdims=True)
        weights = [jnp.exp2((tile - top) * to_exponent) for tile in tiles]
        inverse = 1.0 / jnp.sum(functools.reduce(jnp.add, weights), axis=0, keepdims=True)
        inverse_ref[n] = inverse
        weights = [w.astype(jnp.bfloat16) for w in weights]
        near = weights[span - 1] * near_part
        weights[span - 1] = weights[span - 1] - near
        mixed_ref[n] = matmul(own_value_ref[n * PAIR // group], near) * inverse
        for d in range(span):
            weight_ref[n, d * length : (d + 1) * length] = weights[d]


def mix_kernel(cycle, weight_ref, mixed_ref, inverse_ref, *refs):
    out_hbm, stage_ref, out_sem = refs[-3:]
    value_refs = refs[:-4]
    pairs = weight_ref.shape[0]
    width = mixed_ref.shape[1]
    kv_heads = value_refs[0].shape[1] // width
    group_pairs = pairs // kv_heads

    @pl.when(my_stretch(cycle) > 0)
    def _():
        values, held, ready = [], [], []

        def mixed_pair(n):
            g = n // group_pairs
            if g == len(values):
                parts = [ref[:, columns_of(g, width)].T for ref in value_refs]
                values.append(jnp.concatenate(parts, axis=1))
            return (matmul(values[g], weight_ref[n]) * inverse_ref[n] + mixed_ref[n]).astype(jnp.bfloat16)

        def store_pair(n, mixed):
            put_pair(stage_ref, n, 0, mixed)
            ready.append(n)
            if n in STORE_AFTER or n == pairs - 1:
                for m in ready:
                    start_store(stage_ref, out_hbm, out_sem, m)
                ready.clear()

        for n in range(pairs):
            held.append((n, mixed_pair(n)))
            if len(held) > LAG:
                store_pair(*held.pop(0))
        for item in held:
            store_pair(*item)
        wait_stores(stage_ref, out_sem)


def local(query_proj, key_proj, value_projection, query_gain, key_gain):
    cycle = lax.axis_size("blk")
    span = max(1, cycle // 64)
    length, query_width = query_proj.shape
    kv_width = key_proj.shape[1]
    width = query_gain.shape[0]
    heads = query_width // width
    kv_heads = kv_width // width
    params = pltpu.CompilerParams(vmem_limit_bytes=VMEM_LIMIT)
    vmem = pl.BlockSpec(memory_space=pltpu.VMEM)
    hbm = pl.BlockSpec(memory_space=pltpu.HBM)

    routes = [forward_route(d, cycle) for d in range(1, span + 1)]
    far_keys = [lax.ppermute(key_proj, ("blk", "uly"), route) for route in routes]
    far_values = [lax.ppermute(value_projection, ("blk", "uly"), route) for route in routes]

    base, offset = rotary_tables(2 * cycle, span, length, width)
    operands = (query_proj, key_proj, value_projection, query_gain[None], key_gain[None], base, offset)
    rotated, scores, tables, values, out = pl.pallas_call(
        functools.partial(local_kernel, cycle, span),
        in_specs=[hbm] * 7,
        out_specs=[vmem] * 4 + [hbm],
        out_shape=[
            pltpu.VMEM((heads, length, width), jnp.bfloat16),
            pltpu.VMEM((heads // PAIR, length, PAIR * length), jnp.float32),
            pltpu.VMEM((span, 2, length, width), jnp.float32),
            pltpu.VMEM((kv_heads, width, length), jnp.bfloat16),
            jax.ShapeDtypeStruct(query_proj.shape, jnp.bfloat16),
        ],
        scratch_shapes=[
            pltpu.VMEM((kv_heads, length, query_width // kv_heads), jnp.bfloat16),
            pltpu.VMEM((length, kv_width), jnp.bfloat16),
            pltpu.VMEM((length, kv_width), jnp.bfloat16),
            pltpu.VMEM((1, width), jnp.float32),
            pltpu.VMEM((1, width), jnp.float32),
            pltpu.VMEM(base.shape[1:], jnp.float32),
            pltpu.VMEM(offset.shape, jnp.float32),
            pltpu.SemaphoreType.DMA((5,)),
            pltpu.SemaphoreType.DMA((kv_heads,)),
            pltpu.SemaphoreType.DMA,
            pltpu.VMEM((kv_heads, length, query_width // kv_heads), jnp.bfloat16),
            pltpu.SemaphoreType.DMA,
        ],
        compiler_params=params,
        name="local_scores",
    )(*[pltpu.with_memory_space_constraint(x, pltpu.HBM) for x in operands])
    partial = pl.pallas_call(
        functools.partial(weight_kernel, cycle, span),
        in_specs=[vmem] * (4 + span),
        out_specs=[vmem] * 3,
        out_shape=[
            pltpu.VMEM((heads // PAIR, span * length, PAIR * length), jnp.bfloat16),
            pltpu.VMEM((heads // PAIR, width, PAIR * length), jnp.float32),
            pltpu.VMEM((heads // PAIR, 1, PAIR * length), jnp.float32),
        ],
        compiler_params=params,
        name="weights",
    )(rotated, scores, tables, values, *far_keys)
    return pl.pallas_call(
        functools.partial(mix_kernel, cycle),
        in_specs=[vmem] * (3 + span) + [hbm],
        out_specs=hbm,
        out_shape=jax.ShapeDtypeStruct(query_proj.shape, jnp.bfloat16),
        input_output_aliases={3 + span: 0},
        scratch_shapes=[
            pltpu.VMEM((heads // PAIR, length, PAIR * width), jnp.bfloat16),
            pltpu.SemaphoreType.DMA,
        ],
        compiler_params=params,
        name="mix_values",
    )(*partial, *far_values, out)


def solution(mesh):
    placed = P(("groups", "blk", "uly"), None)
    return jax.shard_map(
        local,
        mesh=mesh,
        in_specs=(placed, placed, placed, P(), P()),
        out_specs=placed,
        check_vma=False,
    )
```

```python
import functools
import math

import jax
import jax.numpy as jnp
import numpy as np
from jax import lax
from jax.experimental import pallas as pl
from jax.experimental.pallas import tpu as pltpu
from jax.sharding import PartitionSpec as P

NEG_FILL = -1e30
ROPE_BASE = 1000000.0
EPSILON = 1e-06
PAIR = 2
LAG = 1
STORE_AFTER = (0, 1, 3, 6, 9, 12, 14)
VMEM_LIMIT = 16 * 1024 * 1024


def stretch_device(stretch, cycle):
    return 2 * stretch if stretch < cycle else 2 * (2 * cycle - 1 - stretch) + 1


def forward_route(distance, cycle):
    total = 2 * cycle
    return [
        (stretch_device(s, cycle), stretch_device((s + distance) % total, cycle))
        for s in range(total)
    ]


def rotary_tables(stretches, span, length, width):
    half = width // 2
    frequency = ROPE_BASE ** (-2.0 * np.arange(half, dtype=np.float64) / width)
    before = np.maximum(np.arange(stretches)[:, None] - np.arange(span + 1), 0).astype(np.float64)
    base = (before * length)[:, :, None] * frequency
    offset = np.arange(length, dtype=np.float64)[:, None] * frequency
    base = np.concatenate([np.cos(base), np.sin(base)], axis=-1)
    offset = np.concatenate([np.cos(offset), np.sin(offset)], axis=-1)
    return base.astype(np.float32), offset.astype(np.float32)


def my_stretch(cycle):
    block = lax.axis_index("blk")
    return jnp.where(lax.axis_index("uly") == 0, block, 2 * cycle - 1 - block)


def spread(packed):
    half = packed.shape[-1] // 2
    first = lax.broadcasted_iota(jnp.int32, packed.shape, 1) < half
    turned = pltpu.roll(packed, half, 1)
    return jnp.where(first, packed, turned), jnp.where(first, turned, packed)


def gained_tables(base, offset, gain):
    width = gain.shape[-1]
    half = width // 2
    gain = gain * math.sqrt(width)
    turned_gain = pltpu.roll(gain, half, 1)
    turned_gain = jnp.where(lax.broadcasted_iota(jnp.int32, gain.shape, 1) < half, -turned_gain, turned_gain)
    (base_cos, base_sin), (cosine, sine) = base, offset
    return gain * (base_cos * cosine - base_sin * sine), turned_gain * (base_sin * cosine + base_cos * sine)


def half_turn(width):
    rows = lax.broadcasted_iota(jnp.int32, (width, width), 0)
    columns = lax.broadcasted_iota(jnp.int32, (width, width), 1)
    swapped = jnp.where(columns < width // 2, columns + width // 2, columns - width // 2)
    return (rows == swapped).astype(jnp.float32).astype(jnp.bfloat16)


def rotate_head(raw, cosine, sine, swap):
    values = raw.astype(jnp.float32)
    width = values.shape[-1]
    square_sum = jnp.sum(values * values, axis=-1, keepdims=True)
    turned = values * cosine + matmul(raw, swap) * sine
    return (turned * lax.rsqrt(square_sum + width * EPSILON)).astype(jnp.bfloat16)


def columns_of(block, width):
    if isinstance(block, int):
        return slice(block * width, (block + 1) * width)
    return pl.ds(pl.multiple_of(block * width, width), width)


def matmul(left, right):
    return jnp.dot(left, right, preferred_element_type=jnp.float32)


def matmul_t(left, right):
    return lax.dot_general(left, right, (((1,), (1,)), ((), ())), preferred_element_type=jnp.float32)


def pair_positions(length):
    shape = (length, PAIR * length)
    columns = lax.broadcasted_iota(jnp.int32, shape, 1)
    return lax.broadcasted_iota(jnp.int32, shape, 0), lax.rem(columns, length)


def put_pair(stage_ref, g, n, mixed):
    width = mixed.shape[0]
    turned = mixed.T
    length = turned.shape[0] // PAIR
    for i in range(PAIR):
        stage_ref[g, :, columns_of(n * PAIR + i, width)] = turned[i * length : (i + 1) * length]


def start_store(stage_ref, out_hbm, out_sem, g):
    place = columns_of(g, stage_ref.shape[2])
    pltpu.make_async_copy(stage_ref.at[g], out_hbm.at[:, place], out_sem).start()


def wait_stores(stage_ref, out_sem):
    pltpu.make_async_copy(stage_ref, stage_ref, out_sem).wait()


def local_kernel(
    cycle,
    span,
    q_hbm,
    k_hbm,
    v_hbm,
    q_gain_hbm,
    k_gain_hbm,
    base_hbm,
    offset_hbm,
    rotated_ref,
    score_ref,
    table_ref,
    value_ref,
    out_hbm,
    q_ref,
    k_ref,
    v_ref,
    q_gain_ref,
    k_gain_ref,
    base_ref,
    offset_ref,
    small_sem,
    q_sem,
    v_sem,
    stage_ref,
    out_sem,
):
    heads, length, width = rotated_ref.shape
    kv_heads = k_ref.shape[1] // width
    group = heads // kv_heads
    stretch = my_stretch(cycle)
    smalls = [
        pltpu.make_async_copy(source, target, small_sem.at[i])
        for i, (source, target) in enumerate(
            [
                (q_gain_hbm, q_gain_ref),
                (k_gain_hbm, k_gain_ref),
                (base_hbm.at[stretch], base_ref),
                (offset_hbm, offset_ref),
                (k_hbm, k_ref),
            ]
        )
    ]
    for copy in smalls:
        copy.start()

    def q_copy(g):
        return pltpu.make_async_copy(q_hbm.at[:, columns_of(g, group * width)], q_ref.at[g], q_sem.at[g])

    for g in range(kv_heads):
        q_copy(g).start()
    v_copy = pltpu.make_async_copy(v_hbm, v_ref, v_sem)
    v_copy.start()
    for copy in smalls:
        copy.wait()

    k_gain = k_gain_ref[...]
    bases = [spread(base_ref[d : d + 1]) for d in range(span + 1)]
    offset = spread(offset_ref[...])
    q_cos, q_sin = gained_tables(bases[0], offset, q_gain_ref[...])
    k_cos, k_sin = gained_tables(bases[0], offset, k_gain)
    for d in range(span):
        table_ref[d, 0], table_ref[d, 1] = gained_tables(bases[d + 1], offset, k_gain)
    swap = half_turn(width)
    keys = [rotate_head(k_ref[:, columns_of(g, width)], k_cos, k_sin, swap) for g in range(kv_heads)]

    def score(g):
        for n in range(g * group // PAIR, (g + 1) * group // PAIR):
            queries = rotated_ref[n * PAIR : (n + 1) * PAIR].reshape(PAIR * length, width)
            score_ref[n] = matmul_t(keys[g], queries)

    first = 0
    for count in [2, 2]:
        some = range(first, first + count)
        for g in some:
            q_copy(g).wait()
        for g in some:
            for i in range(group):
                rotated_ref[g * group + i] = rotate_head(q_ref[g, :, i * width : (i + 1) * width], q_cos, q_sin, swap)
        for g in range(max(first - 1, 0), first + count - 1):
            score(g)
        first += count
    score(kv_heads - 1)
    v_copy.wait()
    for g in range(kv_heads):
        value_ref[g] = v_ref[:, columns_of(g, width)].T

    @pl.when(stretch == 0)
    def _():
        keys_at, queries_at = pair_positions(length)
        own = keys_at <= queries_at
        to_exponent = math.log2(math.e) / math.sqrt(width)
        for g in range(kv_heads):
            for n in range(group // PAIR):
                tile = jnp.where(own, score_ref[g * group // PAIR + n], NEG_FILL)
                weights = jnp.exp2((tile - jnp.max(tile, axis=0, keepdims=True)) * to_exponent)
                inverse = 1.0 / jnp.sum(weights, axis=0, keepdims=True)
                mixed = matmul(value_ref[g], weights.astype(jnp.bfloat16))
                put_pair(stage_ref, g, n, (mixed * inverse).astype(jnp.bfloat16))
            start_store(stage_ref, out_hbm, out_sem, g)
        wait_stores(stage_ref, out_sem)


def weight_kernel(cycle, span, *refs):
    @pl.when(my_stretch(cycle) > 0)
    def _():
        later_weights(cycle, span, *refs)


def later_weights(cycle, span, rotated_ref, score_ref, table_ref, *refs):
    key_refs = refs[:span]
    weight_ref, inverse_ref = refs[span:]
    heads, length, width = rotated_ref.shape
    kv_heads = key_refs[0].shape[1] // width
    group = heads // kv_heads
    stretch = my_stretch(cycle)
    swap = half_turn(width)
    to_exponent = math.log2(math.e) / math.sqrt(width)
    rows = lax.broadcasted_iota(jnp.int32, (length, length), 0)
    columns = lax.broadcasted_iota(jnp.int32, (length, length), 1)
    own = rows <= columns
    near_part = own.astype(jnp.float32).astype(jnp.bfloat16)
    near_part = jnp.concatenate([near_part] * PAIR, axis=1)
    keys = [
        [
            rotate_head(key_refs[d][:, columns_of(g, width)], table_ref[d, 0], table_ref[d, 1], swap)
            for d in range(span)
        ]
        for g in range(kv_heads)
    ]
    for n in range(heads // PAIR):
        queries = rotated_ref[n * PAIR : (n + 1) * PAIR].reshape(PAIR * length, width)
        far = [matmul_t(key, queries) for key in keys[n * PAIR // group]]
        if span > 1:
            far = [jnp.where(stretch > d, far[d], NEG_FILL) for d in range(span)]
        merged = []
        for i in range(PAIR):
            place = columns_of(i, length)
            merged.append(jnp.where(own, score_ref[n, :, place], far[span - 1][:, place]))
        tiles = [*far[: span - 1], jnp.concatenate(merged, axis=1)]
        top = jnp.max(functools.reduce(jnp.maximum, tiles), axis=0, keepdims=True)
        weights = [jnp.exp2((tile - top) * to_exponent) for tile in tiles]
        inverse = 1.0 / jnp.sum(functools.reduce(jnp.add, weights), axis=0, keepdims=True)
        inverse_ref[n] = inverse
        weights = [w.astype(jnp.bfloat16) for w in weights]
        near = weights[span - 1] * near_part
        weights[span - 1] = weights[span - 1] - near
        for d, part in enumerate([near, *weights]):
            weight_ref[n, d * length : (d + 1) * length] = part


def mix_kernel(cycle, weight_ref, inverse_ref, own_value_ref, *refs):
    out_hbm, stage_ref, out_sem = refs[-3:]
    value_refs = refs[:-4]
    pairs = weight_ref.shape[0]
    kv_heads, width, _ = own_value_ref.shape
    group_pairs = pairs // kv_heads

    @pl.when(my_stretch(cycle) > 0)
    def _():
        values, held, ready = [], [], []

        def mixed_pair(n):
            g = n // group_pairs
            if g == len(values):
                parts = [ref[:, columns_of(g, width)].T for ref in value_refs]
                values.append(jnp.concatenate([own_value_ref[g], *parts], axis=1))
            return (matmul(values[g], weight_ref[n]) * inverse_ref[n]).astype(jnp.bfloat16)

        def store_pair(n, mixed):
            put_pair(stage_ref, n, 0, mixed)
            ready.append(n)
            if n in STORE_AFTER or n == pairs - 1:
                for m in ready:
                    start_store(stage_ref, out_hbm, out_sem, m)
                ready.clear()

        for n in range(pairs):
            held.append((n, mixed_pair(n)))
            if len(held) > LAG:
                store_pair(*held.pop(0))
        for item in held:
            store_pair(*item)
        wait_stores(stage_ref, out_sem)


def local(query_proj, key_proj, value_projection, query_gain, key_gain):
    cycle = lax.axis_size("blk")
    span = max(1, cycle // 64)
    length, query_width = query_proj.shape
    kv_width = key_proj.shape[1]
    width = query_gain.shape[0]
    heads = query_width // width
    kv_heads = kv_width // width
    params = pltpu.CompilerParams(vmem_limit_bytes=VMEM_LIMIT)
    vmem = pl.BlockSpec(memory_space=pltpu.VMEM)
    hbm = pl.BlockSpec(memory_space=pltpu.HBM)

    routes = [forward_route(d, cycle) for d in range(1, span + 1)]
    far_keys = [lax.ppermute(key_proj, ("blk", "uly"), route) for route in routes]
    far_values = [lax.ppermute(value_projection, ("blk", "uly"), route) for route in routes]

    base, offset = rotary_tables(2 * cycle, span, length, width)
    operands = (query_proj, key_proj, value_projection, query_gain[None], key_gain[None], base, offset)
    rotated, scores, tables, values, out = pl.pallas_call(
        functools.partial(local_kernel, cycle, span),
        in_specs=[hbm] * 7,
        out_specs=[vmem] * 4 + [hbm],
        out_shape=[
            pltpu.VMEM((heads, length, width), jnp.bfloat16),
            pltpu.VMEM((heads // PAIR, length, PAIR * length), jnp.float32),
            pltpu.VMEM((span, 2, length, width), jnp.float32),
            pltpu.VMEM((kv_heads, width, length), jnp.bfloat16),
            jax.ShapeDtypeStruct(query_proj.shape, jnp.bfloat16),
        ],
        scratch_shapes=[
            pltpu.VMEM((kv_heads, length, query_width // kv_heads), jnp.bfloat16),
            pltpu.VMEM((length, kv_width), jnp.bfloat16),
            pltpu.VMEM((length, kv_width), jnp.bfloat16),
            pltpu.VMEM((1, width), jnp.float32),
            pltpu.VMEM((1, width), jnp.float32),
            pltpu.VMEM(base.shape[1:], jnp.float32),
            pltpu.VMEM(offset.shape, jnp.float32),
            pltpu.SemaphoreType.DMA((5,)),
            pltpu.SemaphoreType.DMA((kv_heads,)),
            pltpu.SemaphoreType.DMA,
            pltpu.VMEM((kv_heads, length, query_width // kv_heads), jnp.bfloat16),
            pltpu.SemaphoreType.DMA,
        ],
        compiler_params=params,
        name="local_scores",
    )(*[pltpu.with_memory_space_constraint(x, pltpu.HBM) for x in operands])
    weights, inverse = pl.pallas_call(
        functools.partial(weight_kernel, cycle, span),
        in_specs=[vmem] * (3 + span),
        out_specs=[vmem] * 2,
        out_shape=[
            pltpu.VMEM((heads // PAIR, (span + 1) * length, PAIR * length), jnp.bfloat16),
            pltpu.VMEM((heads // PAIR, 1, PAIR * length), jnp.float32),
        ],
        compiler_params=params,
        name="weights",
    )(rotated, scores, tables, *far_keys)
    return pl.pallas_call(
        functools.partial(mix_kernel, cycle),
        in_specs=[vmem] * (3 + span) + [hbm],
        out_specs=hbm,
        out_shape=jax.ShapeDtypeStruct(query_proj.shape, jnp.bfloat16),
        input_output_aliases={3 + span: 0},
        scratch_shapes=[
            pltpu.VMEM((heads // PAIR, length, PAIR * width), jnp.bfloat16),
            pltpu.SemaphoreType.DMA,
        ],
        compiler_params=params,
        name="mix_values",
    )(weights, inverse, values, *far_values, out)


def solution(mesh):
    placed = P(("groups", "blk", "uly"), None)
    return jax.shard_map(
        local,
        mesh=mesh,
        in_specs=(placed, placed, placed, P(), P()),
        out_specs=placed,
        check_vma=False,
    )
```
